256 devices in a mesh: dp: 32 (over y, x, core), proto: 8 (over z).
Axes of the slice: x: 4, y: 4, z: 8, core: 2. Of those that a mesh axis runs over, the one named last changes fastest.
Arguments:
- teacher_patches: bfloat16 [24576, 256], P('dp'), may hold values from -8 to 8
- student_patches: bfloat16 [24576, 256], P('dp'), may hold values from -6 to 6
- mask_index: int32 [12288], P('dp'), may hold values from 0 to 767
- teacher_weight: bfloat16 [256, 65536], P(None, 'proto'), may hold values from -8 to 8
- student_weight: bfloat16 [256, 65536], P(None, 'proto'), may hold values from -0.375 to 0.375
Outputs:
- loss: float32 [12288], P('dp')
- grad_weight: float32 [256, 65536], P('dp', 'proto')
- grad_patches: float32 [24576, 256], P('dp')
The draws below stay inside these ranges and needn't reach their ends.
Inputs may be any that keep to these rules, and one draw needn't show every extreme that they name: `mask_index`: entries may repeat within a block of 384 rows.
All inputs are finite; a program needn't handle non-finite values.
Results may differ from the reference program's by a relative error of at most 0.001.
The reference program's roundings to bfloat16 on the way (of `teacher_unit`, `student_unit`, `teacher_proto`, `student_proto` and `grad_logits`) count: a program that leaves them out, or rounds other values in their place, can miss the bound.
Values sent between devices are 32-bit elements; how exact they have to be, the bound alone decides.
A program may use at most 128 MiB of HBM per device.

```python
import jax
import jax.numpy as jnp
from jax import lax

BOT = 256
PROTOS = 65536
ROWS_DEV = 384
ITERS = 3
PATCH_DEV = 768
ROWS = 12288
PATCHES = 24576
N_DP = 32


cluster_count = 8


def cluster_directions(key):
    return jax.random.normal(key, (cluster_count, BOT), jnp.float32)


def skewed_ids(key, amount):
    first_key, second_key = jax.random.split(key)
    first_draw = jax.random.randint(first_key, (amount,), 0, cluster_count)
    second_draw = jax.random.randint(second_key, (amount,), 0, cluster_count)
    return jnp.minimum(first_draw, second_draw)


def draw_teacher_patches(key, part):
    directions = cluster_directions(key)
    key = jax.random.fold_in(key, 17)
    label_key, amplitude_key, jitter_key = jax.random.split(key, 3)
    centers = jnp.take(directions, skewed_ids(label_key, PATCHES), axis=0)
    amplitude = jax.random.uniform(amplitude_key, (PATCHES, 1), jnp.float32, 0.45, 0.9)
    jitter = jax.random.normal(jitter_key, (PATCHES, BOT), jnp.float32)
    values = amplitude * centers + jitter
    return jnp.clip(values, -8.0, 8.0).astype(jnp.bfloat16)


def draw_teacher_weight(key, part):
    directions = cluster_directions(key)
    key = jax.random.fold_in(key, 29)
    label_key, amplitude_key, jitter_key = jax.random.split(key, 3)
    labels = cluster_count - 1 - skewed_ids(label_key, PROTOS)
    centers = jnp.take(directions, labels, axis=0).T
    amplitude = jax.random.uniform(amplitude_key, (1, PROTOS), jnp.float32, 0.45, 0.9)
    jitter = jax.random.normal(jitter_key, (BOT, PROTOS), jnp.float32)
    values = amplitude * centers + jitter
    return jnp.clip(values, -8.0, 8.0).astype(jnp.bfloat16)


def place_ends(entries, rng, least, high):
    longest = entries.shape.index(max(entries.shape))
    spots = []
    for shift in (0, 1):
        where = [jax.random.randint(jax.random.fold_in(rng, axis), (), 0, length) for axis, length in enumerate(entries.shape)]
        where[longest] = (where[longest] + shift) % entries.shape[longest]
        spots.append(tuple(where))
    return entries.at[spots[0]].set(least).at[spots[1]].set(high)


def steps_of(key, extent, cuts, least, largest):
    level, own = 1.0, jax.random.fold_in(key, 6)
    for axis_at, shards_of in cuts:
        steps = jnp.exp(jax.random.uniform(jax.random.fold_in(own, axis_at), (shards_of,), jnp.float32, least / len(cuts), largest / len(cuts)))
        level = level * jnp.repeat(steps, extent[axis_at] // shards_of).reshape([-1 if axis == axis_at else 1 for axis in range(len(extent))])
    return level


def gaussian(key, shape, deviation, bound, shards=(), held_as=jnp.bfloat16):
    result = deviation * jax.random.normal(key, shape, jnp.float32)
    if shards:
        result = result * steps_of(key, shape, shards, -0.22, 0.18)
    return jnp.clip(result, -bound, bound).astype(held_as)


def setup_inputs(seed: int = 0) -> dict:
    key_list = jax.random.split(jax.random.key(seed), 6)
    return {
        "teacher_patches": draw_teacher_patches(jax.random.fold_in(key_list[5], 71), 0),
        "student_patches": gaussian(key_list[1], (PATCHES, BOT), 1.0, 6.0, ((0, 32),)),
        "mask_index": place_ends(jax.random.randint(key_list[2], (ROWS,), 0, PATCH_DEV), jax.random.fold_in(key_list[2], 1), 0, PATCH_DEV - 1).astype(jnp.int32),
        "teacher_weight": draw_teacher_weight(jax.random.fold_in(key_list[5], 71), 0),
        "student_weight": gaussian(key_list[4], (BOT, PROTOS), BOT ** -0.5, 0.375, ((1, 8),)),
    }


epsilon = 1e-06
TEACHER_TEMP = 0.07
STUDENT_TEMP = 0.1

def normalized_rows(values):
    wide = values.astype(jnp.float32)
    inverse = lax.rsqrt(lax.optimization_barrier(jnp.sum(wide * wide, axis=1, keepdims=True)) + epsilon)
    return ((wide * inverse).astype(jnp.bfloat16), inverse, wide)

def normalized_columns(values):
    wide = values.astype(jnp.float32)
    inverse = lax.rsqrt(lax.optimization_barrier(jnp.sum(wide * wide, axis=0, keepdims=True)) + epsilon)
    return ((wide * inverse).astype(jnp.bfloat16), inverse, wide)

def reference(teacher_patches, student_patches, mask_index, teacher_weight, student_weight):
    rows_total = ROWS_DEV * N_DP
    index = jnp.arange(rows_total, dtype=jnp.int32) // ROWS_DEV * PATCH_DEV + mask_index.astype(jnp.int32)
    teacher_rows = jnp.take(teacher_patches, index, axis=0)
    student_rows = jnp.take(student_patches, index, axis=0)
    teacher_unit = normalized_rows(teacher_rows)[0]
    student_unit, row_inverse, student_wide = normalized_rows(student_rows)
    teacher_proto = normalized_columns(teacher_weight)[0]
    student_proto, column_inverse, weight_wide = normalized_columns(student_weight)
    teacher_blocks = teacher_unit.reshape(N_DP, ROWS_DEV, BOT)
    student_blocks = student_unit.reshape(N_DP, ROWS_DEV, BOT)

    def teacher_block(block):
        return jnp.exp(jnp.dot(block, teacher_proto, preferred_element_type=jnp.float32) / TEACHER_TEMP)

    def column_pass(scales):

        def accumulate(total, pair):
            block, scale = pair
            return (total + jnp.dot(scale, teacher_block(block), precision=lax.Precision.HIGHEST), None)
        total, unused = lax.scan(accumulate, jnp.zeros((PROTOS,), jnp.float32), (teacher_blocks, scales))
        return total

    def row_pass(col_scale):
        return lax.map(lambda block: jnp.dot(teacher_block(block), col_scale, precision=lax.Precision.HIGHEST), teacher_blocks)
    row_scale = jnp.ones((N_DP, ROWS_DEV), jnp.float32)
    col_scale = jnp.ones((PROTOS,), jnp.float32)
    for sweep in range(ITERS):
        col_sum = col_scale * column_pass(row_scale)
        col_scale = col_scale / (col_sum * PROTOS)
        row_sum = row_scale * row_pass(col_scale)
        row_scale = row_scale / (row_sum * rows_total)

    def student_total(block):
        return lax.optimization_barrier(jnp.sum(jnp.exp(jnp.dot(block, student_proto, preferred_element_type=jnp.float32) / STUDENT_TEMP), axis=1))
    totals = lax.map(student_total, student_blocks)

    def backward(proto_grad, items):
        tblock, sblock, scale, total = items
        logits = jnp.dot(sblock, student_proto, preferred_element_type=jnp.float32) / STUDENT_TEMP
        student_exp = jnp.exp(logits)
        targets = (rows_total * scale)[:, None] * teacher_block(tblock) * col_scale[None, :]
        row_loss = -lax.optimization_barrier(jnp.sum(targets * (logits - jnp.log(total)[:, None]), axis=1))
        grad_logits = ((student_exp / total[:, None] - targets) / (rows_total * STUDENT_TEMP)).astype(jnp.bfloat16)
        proto_grad = proto_grad + lax.dot_general(sblock, grad_logits, (((0,), (0,)), ((), ())), preferred_element_type=jnp.float32)
        feature = lax.dot_general(grad_logits, student_proto, (((1,), (1,)), ((), ())), preferred_element_type=jnp.float32)
        return (proto_grad, (feature, row_loss))
    start = jnp.zeros((BOT, PROTOS), jnp.float32)
    proto_grad, (features, row_losses) = lax.scan(backward, start, (teacher_blocks, student_blocks, row_scale, totals))
    loss = row_losses.reshape(rows_total)
    grad_weight = column_inverse * proto_grad - weight_wide * column_inverse ** 3 * lax.optimization_barrier(jnp.sum(weight_wide * proto_grad, axis=0, keepdims=True))
    feature_grad = features.reshape(rows_total, BOT)
    row_grad = row_inverse * feature_grad - student_wide * row_inverse ** 3 * lax.optimization_barrier(jnp.sum(student_wide * feature_grad, axis=1, keepdims=True))
    grad_patches = jnp.zeros((PATCH_DEV * N_DP, BOT), jnp.float32).at[index].add(row_grad)
    return (loss, grad_weight, grad_patches)
```

```python
import functools
import math

import jax
import jax.numpy as jnp
from jax import lax
from jax.experimental import pallas as pl
from jax.experimental.pallas import tpu as pltpu
from jax.sharding import PartitionSpec as P

MESH = pl.DeviceIdType.MESH
F32 = jnp.float32
BF16 = jnp.bfloat16

EPS = 1e-06
TEACHER_TEMP = 0.07
STUDENT_TEMP = 0.1
LOG2E = 1.0 / math.log(2.0)

NY, NX, NK, NZ = 4, 4, 2, 8
DP = NY * NX * NK
CHIPS = NY * NX
OWN = 384
ROWS = NK * OWN
WIDTH = 256
PATCH = 768
COLS = 4096
LANES = 128
CH = 512
PARTS = COLS // CH
BLOCK = 256
TOTAL_ROWS = OWN * DP
TOTAL_PROTOS = COLS * NK * NZ
ZROWS = OWN // NZ
GRAD_SCALE = 1.0 / (TOTAL_ROWS * STUDENT_TEMP)
COL_PEERS = [(dy, dx) for dy in range(NY) for dx in range(NX)]
ROW_PEERS = [(dz, dk) for dz in range(NZ) for dk in range(NK)]


def aligned(value, unit):
    return pl.multiple_of(value, unit)


def kernel(
    tpat, spat, midx, tw_hbm, sw_hbm,
    loss_ref, gw_ref, gp_ref,
    tw, sw, tp, sp, cinv, units, tu, su, sut, onehot_t, srow, rinv,
    e_ref, l_ref, part, part2, csend, crecv, cscale, rsend, rrecv, rcol, ltot,
    grad, pg, r1, r2, r3, r4, second, feat, fsib, fz, rg, gwfull, lossrow,
    load_sem, unit_send, unit_recv, col_send, col_recv, row_send, row_recv,
    rs_send, rs_recv, feat_send, feat_recv, gw_send, gw_recv,
):
    dp = lax.axis_index("dp")
    z = lax.axis_index("proto")
    k = lax.rem(dp, NK)
    chip = lax.div(dp, NK)
    x = lax.rem(chip, NX)
    y = lax.div(chip, NX)

    def device(yy, xx, kk, zz):
        return ((yy * NX + xx) * NK + kk, zz)

    def chip_at(dy, dx):
        return device(lax.rem(y + dy, NY), lax.rem(x + dx, NX), k, z)

    def row_at(dz, dk):
        return device(y, x, lax.rem(k + dk, NK), lax.rem(z + dz, NZ))

    sibling = row_at(0, 1)

    def send(src, dst, send_sem, recv_sem, where):
        copy = pltpu.make_async_remote_copy(
            src_ref=src, dst_ref=dst, send_sem=send_sem, recv_sem=recv_sem,
            device_id=where, device_id_type=MESH,
        )
        copy.start()

    def await_bytes(ref, sem):
        pltpu.make_async_copy(ref, ref, sem).wait()

    barrier = pltpu.get_barrier_semaphore()
    for dy, dx in COL_PEERS[1:]:
        pl.semaphore_signal(barrier, inc=1, device_id=chip_at(dy, dx), device_id_type=MESH)
    for dz, dk in ROW_PEERS[1:]:
        pl.semaphore_signal(barrier, inc=1, device_id=row_at(dz, dk), device_id_type=MESH)

    mine = pl.ds(aligned(k * COLS, COLS), COLS)
    load_t = pltpu.make_async_copy(tw_hbm.at[:, mine], tw, load_sem.at[0])
    load_s = pltpu.make_async_copy(sw_hbm.at[:, mine], sw, load_sem.at[1])
    load_t.start()
    load_s.start()

    index = midx[...].reshape(1, OWN)
    index_col = jnp.transpose(jnp.broadcast_to(index.astype(F32), (LANES, OWN)))
    lane = lax.broadcasted_iota(jnp.int32, (OWN, LANES), 1).astype(F32)
    onehot = jnp.concatenate(
        [jnp.where(index_col == lane + float(t * LANES), 1.0, 0.0) for t in range(PATCH // LANES)], axis=1
    ).astype(BF16)
    patch_id = lax.broadcasted_iota(jnp.int32, (PATCH, OWN), 0)
    onehot_t[...] = jnp.where(patch_id == index, 1.0, 0.0).astype(BF16)
    trow = jnp.dot(onehot, tpat[...], preferred_element_type=F32)
    srow_value = jnp.dot(onehot, spat[...], preferred_element_type=F32)
    tinv = lax.rsqrt(jnp.sum(trow * trow, axis=1, keepdims=True) + EPS)
    sinv = lax.rsqrt(jnp.sum(srow_value * srow_value, axis=1, keepdims=True) + EPS)
    srow[...] = srow_value
    rinv[...] = jnp.broadcast_to(sinv, (OWN, LANES))
    units[0, k] = (trow * tinv).astype(BF16).astype(F32)
    units[1, k] = (srow_value * sinv).astype(BF16).astype(F32)

    pl.semaphore_wait(barrier, CHIPS - 1 + NZ * NK - 1)
    for side in range(2):
        send(units.at[side, k], units.at[side, k], unit_send.at[side], unit_recv.at[side], sibling)

    load_t.wait()

    def teacher_columns(j, carry):
        cols = pl.ds(aligned(j * CH, CH), CH)
        wide = tw[:, cols].astype(F32)
        inverse = lax.rsqrt(jnp.sum(wide * wide, axis=0, keepdims=True) + EPS)
        tp[:, cols] = (wide * inverse).astype(BF16)
        return carry

    lax.fori_loop(0, PARTS, teacher_columns, 0)
    load_s.wait()

    def student_columns(j, carry):
        cols = pl.ds(aligned(j * CH, CH), CH)
        wide = sw[:, cols].astype(F32)
        inverse = lax.rsqrt(jnp.sum(wide * wide, axis=0, keepdims=True) + EPS)
        cinv[:, cols] = inverse
        sp[:, cols] = (wide * inverse).astype(BF16)
        return carry

    lax.fori_loop(0, PARTS, student_columns, 0)

    other = lax.rem(k + 1, NK)
    for side in range(2):
        await_bytes(units.at[side, other], unit_recv.at[side])
    for core in range(NK):
        tu[core * OWN:(core + 1) * OWN, :] = units[0, core].astype(BF16)
        su[core * OWN:(core + 1) * OWN, :] = units[1, core].astype(BF16)
        sut[1, :, core * OWN:(core + 1) * OWN] = jnp.transpose(units[1, core]).astype(BF16)
    for xx in range(NX):
        for yy in range(NY):
            to, at = (xx * NY + yy) * 16, (yy * NX + xx) * 16
            sut[0, to:to + 16, :] = sut[1, at:at + 16, :]

    def columns_start(turn):
        for slot, (dy, dx) in enumerate(COL_PEERS):
            if slot:
                send(csend.at[turn], crecv.at[turn, slot], col_send.at[turn], col_recv.at[turn], chip_at(dy, dx))

    def columns_end(turn):
        rest = crecv.at[turn, pl.ds(1, CHIPS - 1)]
        await_bytes(rest, col_recv.at[turn])
        total = csend[turn]
        for slot in range(1, CHIPS):
            total = total + crecv[turn, slot]
        return total

    def rows_start(turn, width):
        cut = pl.ds(0, width)
        for slot, (dz, dk) in enumerate(ROW_PEERS):
            if slot:
                send(
                    rsend.at[turn, :, cut], rrecv.at[turn, slot, :, cut],
                    row_send.at[turn], row_recv.at[turn], row_at(dz, dk),
                )

    def rows_end(turn, width):
        cut = pl.ds(0, width)
        await_bytes(rrecv.at[turn, pl.ds(1, NZ * NK - 1), :, cut], row_recv.at[turn])
        total = rsend[turn, :, 0:width]
        for slot in range(1, NZ * NK):
            total = total + rrecv[turn, slot, :, 0:width]
        return total

    def to_column(row):
        return jnp.transpose(jnp.broadcast_to(row, (LANES, ROWS)))

    def lane_sums(ref):
        return jnp.sum(jnp.transpose(ref[...]), axis=0, keepdims=True)

    def teacher_exp(j, carry):
        cols = pl.ds(aligned(j * CH, CH), CH)
        total = jnp.zeros((1, CH), F32)
        for rb in range(ROWS // BLOCK):
            at = slice(rb * BLOCK, (rb + 1) * BLOCK)
            value = jnp.exp2(
                jnp.dot(tu[at, :], tp[:, cols], preferred_element_type=F32) * (LOG2E / TEACHER_TEMP)
            )
            e_ref[at, cols] = value
            total = total + jnp.sum(value, axis=0, keepdims=True)
        csend[0, :, cols] = total
        return carry

    lax.fori_loop(0, PARTS, teacher_exp, 0)
    columns_start(0)

    part2[...] = jnp.zeros_like(part2)

    def student_logits(j, carry):
        cols = pl.ds(aligned(j * CH, CH), CH)
        for rb in range(ROWS // BLOCK):
            at = slice(rb * BLOCK, (rb + 1) * BLOCK)
            value = jnp.dot(su[at, :], sp[:, cols], preferred_element_type=F32) * (LOG2E / STUDENT_TEMP)
            l_ref[at, cols] = value
            power = jnp.exp2(value)
            total = part2[at, :]
            for t in range(CH // LANES):
                total = total + power[:, t * LANES:(t + 1) * LANES]
            part2[at, :] = total
        return carry

    lax.fori_loop(0, PARTS, student_logits, 0)

    STEP = 64

    def row_pass(with_loss):
        def body(rb, carry):
            at = pl.ds(aligned(rb * STEP, STEP), STEP)
            total = jnp.zeros((STEP, LANES), F32)
            cross = jnp.zeros((STEP, LANES), F32)
            for t in range(COLS // LANES):
                cut = slice(t * LANES, (t + 1) * LANES)
                value = e_ref[at, cut] * cscale[:, cut]
                total = total + value
                if with_loss:
                    cross = cross + value * l_ref[at, cut]
            part[at, :] = total
            if with_loss:
                part2[at, :] = cross
            return carry

        lax.fori_loop(0, ROWS // STEP, body, 0)

    WIDE = 1024

    def col_pass(turn):
        def body(j, carry):
            def inner(rb, totals):
                at = pl.ds(aligned(rb * STEP, STEP), STEP)
                scale = rcol[at, :]
                out = []
                for t in range(WIDE // LANES):
                    value = e_ref[at, pl.ds(aligned(j * WIDE + t * LANES, LANES), LANES)] * scale
                    out.append(totals[t] + jnp.sum(value.reshape(STEP // 8, 8, LANES), axis=0))
                return tuple(out)

            start = tuple(jnp.zeros((8, LANES), F32) for _ in range(WIDE // LANES))
            totals = lax.fori_loop(0, ROWS // STEP, inner, start)
            for t in range(WIDE // LANES):
                csend[turn, :, pl.ds(aligned(j * WIDE + t * LANES, LANES), LANES)] = jnp.sum(
                    totals[t], axis=0, keepdims=True
                )
            return carry

        lax.fori_loop(0, COLS // WIDE, body, 0)

    cscale[...] = 1.0 / (columns_end(0) * TOTAL_PROTOS)
    rsend[0, :, ROWS:2 * ROWS] = lane_sums(part2)
    row_pass(False)
    rsend[0, :, 0:ROWS] = lane_sums(part)
    rows_start(0, 2 * ROWS)
    both = rows_end(0, 2 * ROWS)
    rcol[...] = to_column(1.0 / (both[:, 0:ROWS] * TOTAL_ROWS))
    col_pass(1)
    columns_start(1)
    log_total = jnp.log(both[:, ROWS:2 * ROWS])
    ltot[...] = to_column((log_total - math.log(GRAD_SCALE)) * LOG2E)
    cscale[...] = 1.0 / (columns_end(1) * TOTAL_PROTOS)
    row_pass(False)
    rsend[1, :, 0:ROWS] = lane_sums(part)
    rows_start(1, ROWS)
    rcol[...] = to_column(1.0 / (rows_end(1, ROWS) * TOTAL_ROWS))
    col_pass(2)
    columns_start(2)
    cscale[...] = 1.0 / (columns_end(2) * TOTAL_PROTOS)
    row_pass(True)
    rsend[2, :, 0:ROWS] = lane_sums(part)
    rsend[2, :, ROWS:2 * ROWS] = lane_sums(part2)
    rows_start(2, 2 * ROWS)
    both = rows_end(2, 2 * ROWS)
    row_sum = both[:, 0:ROWS]
    row_scale = 1.0 / (row_sum * TOTAL_ROWS)
    rcol[...] = to_column(row_scale * (TOTAL_ROWS * GRAD_SCALE))
    target_sum = row_sum * (row_scale * TOTAL_ROWS)
    target_logits = both[:, ROWS:2 * ROWS] * (row_scale * (TOTAL_ROWS / LOG2E))
    lossrow[...] = log_total * target_sum - target_logits

    ahead = {0: (chip_at(0, 1), chip_at(0, 3), x), 1: (chip_at(1, 0), chip_at(3, 0), y)}
    feat[...] = jnp.zeros_like(feat)

    def gradient(j, carry):
        for kind in range(2):
            q = 2 * j + kind
            cols = pl.ds(aligned(q * CH, CH), CH)
            for rb in range(ROWS // BLOCK):
                at = slice(rb * BLOCK, (rb + 1) * BLOCK)
                scale = rcol[at, :]
                shift = ltot[at, :]
                for t in range(CH // LANES):
                    cut = pl.ds(aligned(q * CH + t * LANES, LANES), LANES)
                    probs = jnp.exp2(l_ref[at, cut] - shift)
                    target = e_ref[at, cut] * cscale[:, cut] * scale
                    grad[at, t * LANES:(t + 1) * LANES] = (probs - target).astype(BF16)
            pg[q] = jnp.dot(sut[kind], grad[...], preferred_element_type=F32)
            plus, minus, a = ahead[kind]
            opposite = lax.rem(a + 2, 4) * 64
            ap, am = lax.rem(a + 1, 4) * 64, lax.rem(a + 3, 4) * 64
            send(pg.at[q, pl.ds(aligned(opposite, 32), 32)], r1.at[q, 0], rs_send.at[q, 0], rs_recv.at[q, 0], plus)
            send(pg.at[q, pl.ds(aligned(opposite + 32, 32), 32)], r1.at[q, 1], rs_send.at[q, 0], rs_recv.at[q, 1], minus)
            send(pg.at[q, pl.ds(aligned(ap + 32, 32), 32)], r2.at[q, 0, pl.ds(32, 32)], rs_send.at[q, 0], rs_recv.at[q, 2], plus)
            send(pg.at[q, pl.ds(aligned(am, 32), 32)], r2.at[q, 1, pl.ds(0, 32)], rs_send.at[q, 0], rs_recv.at[q, 2], minus)
            inner = jnp.zeros((1, CH), F32)
            for yy in range(NY):
                for xx in range(NX):
                    at = (yy * NX + xx) * 16
                    to = (xx * NY + yy) * 16 if kind == 0 else at
                    inner = inner + jnp.sum(
                        sw[at:at + 16, cols].astype(F32) * pg[q, to:to + 16, :], axis=0, keepdims=True
                    )
            csend[3, :, cols] = inner
            feat[...] += lax.dot_general(
                grad[...], sp[:, cols], (((1,), (1,)), ((), ())), preferred_element_type=F32
            )
        return carry

    lax.fori_loop(0, PARTS // 2, gradient, 0)
    send(feat.at[pl.ds(aligned(other * OWN, OWN), OWN)], fsib, feat_send.at[0], feat_recv.at[0], sibling)
    columns_start(3)

    def first_forward(j, carry):
        for kind in range(2):
            q = 2 * j + kind
            plus, minus, a = ahead[kind]
            ap = aligned(lax.rem(a + 1, 4) * 64, 32)
            am = aligned(lax.rem(a + 3, 4) * 64 + 32, 32)
            await_bytes(r1.at[q, 0], rs_recv.at[q, 0])
            pg[q, pl.ds(ap, 32), :] = pg[q, pl.ds(ap, 32), :] + r1[q, 0]
            send(pg.at[q, pl.ds(ap, 32)], r2.at[q, 0, pl.ds(0, 32)], rs_send.at[q, 0], rs_recv.at[q, 2], plus)
            await_bytes(r1.at[q, 1], rs_recv.at[q, 1])
            pg[q, pl.ds(am, 32), :] = pg[q, pl.ds(am, 32), :] + r1[q, 1]
            send(pg.at[q, pl.ds(am, 32)], r2.at[q, 1, pl.ds(32, 32)], rs_send.at[q, 0], rs_recv.at[q, 2], minus)
        return carry

    lax.fori_loop(0, PARTS // 2, first_forward, 0)

    own_rows = pl.ds(aligned(k * OWN, OWN), OWN)
    await_bytes(fsib, feat_recv.at[0])
    feat[own_rows, :] = feat[own_rows, :] + fsib[...]
    for dz in range(1, NZ):
        to = lax.rem(z + dz, NZ)
        rows = pl.ds(aligned(k * OWN + to * ZROWS, ZROWS), ZROWS)
        send(feat.at[rows], fz.at[dz], feat_send.at[1], feat_recv.at[1], row_at(dz, 0))

    def second_start(j, carry):
        for kind in range(2):
            q = 2 * j + kind
            a = ahead[kind][2]
            plus, minus, b = ahead[1 - kind]
            await_bytes(r2.at[q], rs_recv.at[q, 2])
            second[q] = pg[q, pl.ds(aligned(a * 64, 64), 64), :] + r2[q, 0] + r2[q, 1]
            opposite = lax.rem(b + 2, 4) * 16
            bp, bm = lax.rem(b + 1, 4) * 16, lax.rem(b + 3, 4) * 16
            send(second.at[q, pl.ds(aligned(opposite, 8), 8)], r3.at[q, 0], rs_send.at[q, 1], rs_recv.at[q, 3], plus)
            send(second.at[q, pl.ds(aligned(opposite + 8, 8), 8)], r3.at[q, 1], rs_send.at[q, 1], rs_recv.at[q, 4], minus)
            send(second.at[q, pl.ds(aligned(bp + 8, 8), 8)], r4.at[q, 0, pl.ds(8, 8)], rs_send.at[q, 1], rs_recv.at[q, 5], plus)
            send(second.at[q, pl.ds(aligned(bm, 8), 8)], r4.at[q, 1, pl.ds(0, 8)], rs_send.at[q, 1], rs_recv.at[q, 5], minus)
        return carry

    lax.fori_loop(0, PARTS // 2, second_start, 0)

    await_bytes(fz.at[pl.ds(1, NZ - 1)], feat_recv.at[1])
    feature = feat[pl.ds(aligned(k * OWN + z * ZROWS, ZROWS), ZROWS), :]
    for dz in range(1, NZ):
        feature = feature + fz[dz]
    share = pl.ds(aligned(z * ZROWS, ZROWS), ZROWS)
    rows_wide = srow[share, :]
    inverse = rinv[share, 0:1]
    rg[share, :] = inverse * feature - rows_wide * (inverse * inverse * inverse) * jnp.sum(
        rows_wide * feature, axis=1, keepdims=True
    )
    for dz in range(1, NZ):
        send(rg.at[share], rg.at[share], feat_send.at[2], feat_recv.at[2], row_at(dz, 0))

    def second_forward(j, carry):
        for kind in range(2):
            q = 2 * j + kind
            plus, minus, b = ahead[1 - kind]
            bp = aligned(lax.rem(b + 1, 4) * 16, 8)
            bm = aligned(lax.rem(b + 3, 4) * 16 + 8, 8)
            await_bytes(r3.at[q, 0], rs_recv.at[q, 3])
            second[q, pl.ds(bp, 8), :] = second[q, pl.ds(bp, 8), :] + r3[q, 0]
            send(second.at[q, pl.ds(bp, 8)], r4.at[q, 0, pl.ds(0, 8)], rs_send.at[q, 1], rs_recv.at[q, 5], plus)
            await_bytes(r3.at[q, 1], rs_recv.at[q, 4])
            second[q, pl.ds(bm, 8), :] = second[q, pl.ds(bm, 8), :] + r3[q, 1]
            send(second.at[q, pl.ds(bm, 8)], r4.at[q, 1, pl.ds(8, 8)], rs_send.at[q, 1], rs_recv.at[q, 5], minus)
        return carry

    lax.fori_loop(0, PARTS // 2, second_forward, 0)

    chip_rows = pl.ds(aligned(chip * 16, 16), 16)
    inner_total = columns_end(3)
    cscale[...] = inner_total * (cinv[...] * cinv[...] * cinv[...])

    def finish(j, carry):
        for kind in range(2):
            q = 2 * j + kind
            cols = pl.ds(aligned(q * CH, CH), CH)
            b = ahead[1 - kind][2]
            await_bytes(r4.at[q], rs_recv.at[q, 5])
            total = second[q, pl.ds(aligned(b * 16, 16), 16), :] + r4[q, 0] + r4[q, 1]
            value = cinv[:, cols] * total - sw[chip_rows, cols].astype(F32) * cscale[:, cols]
            gwfull[k, 0, :, cols] = value[0:8]
            gwfull[k, 1, :, cols] = value[8:16]
        return carry

    lax.fori_loop(0, PARTS // 2, finish, 0)
    send(gwfull.at[k, other], gwfull.at[k, other], gw_send.at[0], gw_recv.at[0], sibling)

    loss_ref[...] = lossrow[0, pl.ds(aligned(k * OWN, LANES), OWN)]

    await_bytes(rg.at[pl.ds(0, (NZ - 1) * ZROWS)], feat_recv.at[2])
    value = rg[...]
    high = value.astype(BF16)
    value = value - high.astype(F32)
    middle = value.astype(BF16)
    low = (value - middle.astype(F32)).astype(BF16)
    scatter = onehot_t[...]
    gp_ref[...] = (
        jnp.dot(scatter, low, preferred_element_type=F32)
        + jnp.dot(scatter, middle, preferred_element_type=F32)
        + jnp.dot(scatter, high, preferred_element_type=F32)
    )

    await_bytes(gwfull.at[other, k], gw_recv.at[0])
    for core in range(NK):
        gw_ref[:, core * COLS:(core + 1) * COLS] = gwfull[core, k]

    for side in range(2):
        await_bytes(units.at[side, k], unit_send.at[side])
    for turn in range(4):
        await_bytes(crecv.at[turn, pl.ds(1, CHIPS - 1)], col_send.at[turn])
    for turn in range(3):
        cut = pl.ds(0, ROWS if turn == 1 else 2 * ROWS)
        await_bytes(rrecv.at[turn, pl.ds(1, NZ * NK - 1), :, cut], row_send.at[turn])

    def sent(q, carry):
        await_bytes(pg.at[q, pl.ds(0, 192)], rs_send.at[q, 0])
        await_bytes(second.at[q, pl.ds(0, 48)], rs_send.at[q, 1])
        return carry

    lax.fori_loop(0, PARTS, sent, 0)
    await_bytes(fsib, feat_send.at[0])
    await_bytes(fz.at[pl.ds(1, NZ - 1)], feat_send.at[1])
    await_bytes(rg.at[pl.ds(0, (NZ - 1) * ZROWS)], feat_send.at[2])
    await_bytes(gwfull.at[k, other], gw_send.at[0])


def shards(teacher_patches, student_patches, mask_index, teacher_weight, student_weight):
    vmem = pl.BlockSpec(memory_space=pltpu.VMEM)
    hbm = pl.BlockSpec(memory_space=pl.ANY)
    scratch = [
        pltpu.VMEM((WIDTH, COLS), BF16),
        pltpu.VMEM((WIDTH, COLS), BF16),
        pltpu.VMEM((WIDTH, COLS), BF16),
        pltpu.VMEM((WIDTH, COLS), BF16),
        pltpu.VMEM((1, COLS), F32),
        pltpu.VMEM((2, NK, OWN, WIDTH), F32),
        pltpu.VMEM((ROWS, WIDTH), BF16),
        pltpu.VMEM((ROWS, WIDTH), BF16),
        pltpu.VMEM((2, WIDTH, ROWS), BF16),
        pltpu.VMEM((PATCH, OWN), BF16),
        pltpu.VMEM((OWN, WIDTH), F32),
        pltpu.VMEM((OWN, LANES), F32),
        pltpu.VMEM((ROWS, COLS), F32),
        pltpu.VMEM((ROWS, COLS), F32),
        pltpu.VMEM((ROWS, LANES), F32),
        pltpu.VMEM((ROWS, LANES), F32),
        pltpu.VMEM((4, 1, COLS), F32),
        pltpu.VMEM((4, CHIPS, 1, COLS), F32),
        pltpu.VMEM((1, COLS), F32),
        pltpu.VMEM((3, 1, 2 * ROWS), F32),
        pltpu.VMEM((3, NZ * NK, 1, 2 * ROWS), F32),
        pltpu.VMEM((ROWS, LANES), F32),
        pltpu.VMEM((ROWS, LANES), F32),
        pltpu.VMEM((ROWS, CH), BF16),
        pltpu.VMEM((PARTS, WIDTH, CH), F32),
        pltpu.VMEM((PARTS, 2, 32, CH), F32),
        pltpu.VMEM((PARTS, 2, 64, CH), F32),
        pltpu.VMEM((PARTS, 2, 8, CH), F32),
        pltpu.VMEM((PARTS, 2, 16, CH), F32),
        pltpu.VMEM((PARTS, 64, CH), F32),
        pltpu.VMEM((ROWS, WIDTH), F32),
        pltpu.VMEM((OWN, WIDTH), F32),
        pltpu.VMEM((NZ, ZROWS, WIDTH), F32),
        pltpu.VMEM((OWN, WIDTH), F32),
        pltpu.VMEM((NK, NK, 8, COLS), F32),
        pltpu.VMEM((1, ROWS), F32),
        pltpu.SemaphoreType.DMA((2,)),
        pltpu.SemaphoreType.DMA((2,)),
        pltpu.SemaphoreType.DMA((2,)),
        pltpu.SemaphoreType.DMA((4,)),
        pltpu.SemaphoreType.DMA((4,)),
        pltpu.SemaphoreType.DMA((3,)),
        pltpu.SemaphoreType.DMA((3,)),
        pltpu.SemaphoreType.DMA((PARTS, 2)),
        pltpu.SemaphoreType.DMA((PARTS, 6)),
        pltpu.SemaphoreType.DMA((3,)),
        pltpu.SemaphoreType.DMA((3,)),
        pltpu.SemaphoreType.DMA((1,)),
        pltpu.SemaphoreType.DMA((1,)),
    ]
    loss, grad_weight, grad_patches = pl.pallas_call(
        kernel,
        out_shape=(
            jax.ShapeDtypeStruct((OWN,), F32),
            jax.ShapeDtypeStruct((WIDTH // DP, NK * COLS), F32),
            jax.ShapeDtypeStruct((PATCH, WIDTH), F32),
        ),
        in_specs=[vmem, vmem, vmem, hbm, hbm],
        out_specs=(vmem, vmem, vmem),
        scratch_shapes=scratch,
        compiler_params=pltpu.CompilerParams(
            collective_id=0, has_side_effects=True, vmem_limit_bytes=60 * 1024 * 1024
        ),
    )(teacher_patches, student_patches, mask_index, teacher_weight, student_weight)
    return loss, grad_weight, grad_patches


def solution(mesh):
    placed = (P("dp", None), P("dp", None), P("dp"), P(None, "proto"), P(None, "proto"))
    return jax.shard_map(
        shards,
        mesh=mesh,
        in_specs=placed,
        out_specs=(P("dp"), P("dp", "proto"), P("dp", None)),
        check_vma=False,
    )
```

```python
import math

import jax
import jax.numpy as jnp
from jax import lax
from jax.experimental import pallas as pl
from jax.experimental.pallas import tpu as pltpu
from jax.sharding import PartitionSpec as P

MESH = pl.DeviceIdType.MESH
F32 = jnp.float32
BF16 = jnp.bfloat16

EPS = 1e-06
TEACHER_TEMP = 0.07
STUDENT_TEMP = 0.1
LOG2E = 1.0 / math.log(2.0)

NY, NX, NK, NZ = 4, 4, 2, 8
DP = NY * NX * NK
CHIPS = NY * NX
OWN = 384
ROWS = NK * OWN
WIDTH = 256
PATCH = 768
COLS = 4096
LANES = 128
CH = 512
PARTS = COLS // CH
TOTAL_ROWS = OWN * DP
TOTAL_PROTOS = COLS * NK * NZ
ZROWS = OWN // NZ
GRAD_SCALE = 1.0 / (TOTAL_ROWS * STUDENT_TEMP)
COL_PEERS = [(dy, dx) for dy in range(NY) for dx in range(NX)]
ROW_PEERS = [(dz, dk) for dz in range(NZ) for dk in range(NK)]
PAIRS = PARTS // 2
TILES = COLS // LANES
HALF = TILES // 2
RB = 128
STEP = 64
ZHALF = ZROWS // 2
LAG = 2
EARLY = PAIRS // 2
DELAY = 2


def farthest_first(peers, sizes):
    return sorted(peers, key=lambda at: -sum(min(d, n - d) for d, n in zip(at, sizes)))


def aligned(value, unit):
    return pl.multiple_of(value, unit)


def kernel(
    tpat_hbm, spat_hbm, midx, tw_hbm, sw_hbm,
    loss_ref, gw_ref, rg_ref,
    tpat, spat, tw, sw, tp, sp, cinv, units, tu, su, sut, srow, rinv,
    e_ref, l_ref, part, part2, csend, crecv, cscale, rsend, rrecv, rcol, ltot,
    grad, pg, r1, r2, r3, r4, second, feat, fsib, fz, rg, gwfull, lossrow,
    ipart, irecv, inner_all,
    load_sem, unit_send, unit_recv, col_send, col_recv, row_send, row_recv,
    rs_send, rs_recv, feat_send, feat_recv, gw_send, gw_recv, inner_send, inner_recv,
):
    dp = lax.axis_index("dp")
    z = lax.axis_index("proto")
    k = lax.rem(dp, NK)
    chip = lax.div(dp, NK)
    x = lax.rem(chip, NX)
    y = lax.div(chip, NX)
    other = lax.rem(k + 1, NK)

    def device(yy, xx, kk, zz):
        return ((yy * NX + xx) * NK + kk, zz)

    def chip_at(dy, dx):
        return device(lax.rem(y + dy, NY), lax.rem(x + dx, NX), k, z)

    def row_at(dz, dk):
        return device(y, x, lax.rem(k + dk, NK), lax.rem(z + dz, NZ))

    sibling = row_at(0, 1)

    def send(src, dst, send_sem, recv_sem, where):
        copy = pltpu.make_async_remote_copy(
            src_ref=src, dst_ref=dst, send_sem=send_sem, recv_sem=recv_sem,
            device_id=where, device_id_type=MESH,
        )
        copy.start()

    def await_bytes(ref, sem):
        pltpu.make_async_copy(ref, ref, sem).wait()

    leaving = []

    loads = []
    mine = pl.ds(aligned(k * COLS, COLS), COLS)
    for turn, (src, dst) in enumerate(
        ((tpat_hbm, tpat), (tw_hbm.at[:, mine], tw), (spat_hbm, spat), (sw_hbm.at[:, mine], sw))
    ):
        loads.append(pltpu.make_async_copy(src, dst, load_sem.at[turn]))
        loads[-1].start()

    barrier = pltpu.get_barrier_semaphore()
    for dz, dk in farthest_first(ROW_PEERS[1:], (NZ, NK)):
        pl.semaphore_signal(barrier, inc=1, device_id=row_at(dz, dk), device_id_type=MESH)
    for dy, dx in farthest_first(COL_PEERS[1:], (NY, NX)):
        pl.semaphore_signal(barrier, inc=1, device_id=chip_at(dy, dx), device_id_type=MESH)

    def half_rows(core):
        return pl.ds(aligned(core * OWN, LANES), OWN)

    index = midx[...].reshape(1, OWN)
    index_col = jnp.transpose(jnp.broadcast_to(index.astype(F32), (LANES, OWN)))
    lane = lax.broadcasted_iota(jnp.int32, (OWN, LANES), 1).astype(F32)
    onehot = jnp.concatenate(
        [jnp.where(index_col == lane + float(t * LANES), 1.0, 0.0) for t in range(PATCH // LANES)], axis=1
    ).astype(BF16)

    def unit_rows(side, patches, ref):
        rows = jnp.dot(onehot, patches[...], preferred_element_type=F32)
        inverse = lax.rsqrt(jnp.sum(rows * rows, axis=1, keepdims=True) + EPS)
        unit = (rows * inverse).astype(BF16)
        ref[half_rows(k), :] = unit
        units[side, k] = unit.astype(F32)
        return rows, inverse

    loads[0].wait()
    unit_rows(0, tpat, tu)
    loads[2].wait()
    srow_value, sinv = unit_rows(1, spat, su)
    srow[...] = srow_value
    rinv[...] = jnp.broadcast_to(sinv, (OWN, LANES))

    def teacher_columns(j, carry):
        cols = pl.ds(aligned(j * CH, CH), CH)
        wide = tw[:, cols].astype(F32)
        inverse = lax.rsqrt(jnp.sum(wide * wide, axis=0, keepdims=True) + EPS)
        tp[:, cols] = (wide * inverse).astype(BF16)
        return carry

    def student_columns(j, carry):
        cols = pl.ds(aligned(j * CH, CH), CH)
        wide = sw[:, cols].astype(F32)
        inverse = lax.rsqrt(jnp.sum(wide * wide, axis=0, keepdims=True) + EPS)
        for t in range(CH // LANES):
            cinv[pl.ds(j * (CH // LANES) + t, 1), :] = inverse[:, t * LANES:(t + 1) * LANES]
        sp[:, cols] = (wide * inverse).astype(BF16)
        return carry

    def teacher_exp(core, first, last, add):
        def body(j, carry):
            cols = pl.ds(aligned(j * CH, CH), CH)
            total = jnp.zeros((1, CH), F32)
            for rb in range(OWN // RB):
                at = pl.ds(aligned(core * OWN + rb * RB, RB), RB)
                value = jnp.exp2(
                    jnp.dot(tu[at, :], tp[:, cols], preferred_element_type=F32) * (LOG2E / TEACHER_TEMP)
                )
                e_ref[at, cols] = value
                total = total + jnp.sum(value, axis=0, keepdims=True)
            for t in range(CH // LANES):
                row = pl.ds(j * (CH // LANES) + t, 1)
                piece = total[:, t * LANES:(t + 1) * LANES]
                csend[0, row, :] = csend[0, row, :] + piece if add else piece
            return carry

        lax.fori_loop(first, last, body, 0)

    def student_logits(core):
        def body(j, carry):
            cols = pl.ds(aligned(j * CH, CH), CH)
            for rb in range(OWN // RB):
                at = pl.ds(aligned(core * OWN + rb * RB, RB), RB)
                value = jnp.dot(su[at, :], sp[:, cols], preferred_element_type=F32) * (LOG2E / STUDENT_TEMP)
                l_ref[at, cols] = value
                power = jnp.exp2(value)
                total = part2[at, :]
                for t in range(CH // LANES):
                    total = total + power[:, t * LANES:(t + 1) * LANES]
                part2[at, :] = total
            return carry

        lax.fori_loop(0, PARTS, body, 0)

    def columns_start(turn, half):
        cut = pl.ds(half * HALF, HALF)
        for slot, (dy, dx) in enumerate(COL_PEERS):
            if slot:
                send(
                    csend.at[turn, cut], crecv.at[turn, slot, cut],
                    col_send.at[turn, half], col_recv.at[turn, half], chip_at(dy, dx),
                )
        leaving.append((crecv.at[turn, pl.ds(1, CHIPS - 1), cut], col_send.at[turn, half]))

    def columns_end(turn, half):
        cut = pl.ds(half * HALF, HALF)
        await_bytes(crecv.at[turn, pl.ds(1, CHIPS - 1), cut], col_recv.at[turn, half])
        total = csend[turn, cut, :]
        for slot in range(1, CHIPS):
            total = total + crecv[turn, slot, cut, :]
        cscale[cut, :] = 1.0 / (total * TOTAL_PROTOS)

    def rows_start(turn, depth):
        cut = pl.ds(0, depth)
        for slot, (dz, dk) in enumerate(ROW_PEERS):
            if slot:
                send(
                    rsend.at[turn, cut], rrecv.at[turn, slot, cut],
                    row_send.at[turn], row_recv.at[turn], row_at(dz, dk),
                )
        leaving.append((rrecv.at[turn, pl.ds(1, NZ * NK - 1), cut], row_send.at[turn]))

    def rows_end(turn, depth):
        cut = pl.ds(0, depth)
        await_bytes(rrecv.at[turn, pl.ds(1, NZ * NK - 1), cut], row_recv.at[turn])
        total = rsend[turn, cut, :]
        for slot in range(1, NZ * NK):
            total = total + rrecv[turn, slot, cut, :]
        return total

    def to_column(ref, rows):
        for b in range(ROWS // LANES):
            ref[b * LANES:(b + 1) * LANES, :] = jnp.transpose(jnp.broadcast_to(rows[b:b + 1, :], (LANES, LANES)))

    def lane_sums(turn, base, ref):
        for b in range(ROWS // LANES):
            rsend[turn, base + b:base + b + 1, :] = jnp.sum(
                jnp.transpose(ref[b * LANES:(b + 1) * LANES, :]), axis=0, keepdims=True
            )

    def row_pass(half, with_loss):
        def body(rb, carry):
            at = pl.ds(aligned(rb * STEP, STEP), STEP)
            total = part[at, :] if half else jnp.zeros((STEP, LANES), F32)
            if with_loss:
                cross = part2[at, :] if half else jnp.zeros((STEP, LANES), F32)
            for t in range(half * HALF, (half + 1) * HALF):
                cut = slice(t * LANES, (t + 1) * LANES)
                value = e_ref[at, cut] * cscale[t:t + 1, :]
                total = total + value
                if with_loss:
                    cross = cross + value * l_ref[at, cut]
            part[at, :] = total
            if with_loss:
                part2[at, :] = cross
            return carry

        lax.fori_loop(0, ROWS // STEP, body, 0)

    def col_pass(turn, half):
        def body(rb, totals):
            at = pl.ds(aligned(rb * STEP, STEP), STEP)
            scale = rcol[at, :]
            out = []
            for t in range(HALF):
                cut = slice((half * HALF + t) * LANES, (half * HALF + t + 1) * LANES)
                value = e_ref[at, cut] * scale
                out.append(totals[t] + jnp.sum(value.reshape(STEP // 8, 8, LANES), axis=0))
            return tuple(out)

        totals = lax.fori_loop(0, ROWS // STEP, body, tuple(jnp.zeros((8, LANES), F32) for _ in range(HALF)))
        for t in range(HALF):
            row = half * HALF + t
            csend[turn, row:row + 1, :] = jnp.sum(totals[t], axis=0, keepdims=True)

    loads[1].wait()
    lax.fori_loop(0, PARTS, teacher_columns, 0)
    teacher_exp(k, 0, PARTS, False)
    part2[...] = jnp.zeros_like(part2)
    rsend[...] = jnp.zeros_like(rsend)

    pl.semaphore_wait(barrier, CHIPS - 1 + NZ * NK - 1)
    for side in range(2):
        send(units.at[side, k], units.at[side, k], unit_send.at[side], unit_recv.at[side], sibling)
        leaving.append((units.at[side, k], unit_send.at[side]))
    loads[3].wait()
    lax.fori_loop(0, PARTS, student_columns, 0)
    await_bytes(units.at[0, other], unit_recv.at[0])
    tu[half_rows(other), :] = units[0, other].astype(BF16)
    teacher_exp(other, 0, PARTS // 2, True)
    columns_start(0, 0)
    teacher_exp(other, PARTS // 2, PARTS, True)
    columns_start(0, 1)
    await_bytes(units.at[1, other], unit_recv.at[1])
    su[half_rows(other), :] = units[1, other].astype(BF16)
    student_logits(k)
    student_logits(other)
    lane_sums(0, 8, part2)
    for core in range(NK):
        sut[1, :, core * OWN:(core + 1) * OWN] = jnp.transpose(units[1, core]).astype(BF16)
    for xx in range(NX):
        for yy in range(NY):
            to, at = (xx * NY + yy) * 16, (yy * NX + xx) * 16
            sut[0, to:to + 16, :] = sut[1, at:at + 16, :]
    for half in range(2):
        columns_end(0, half)
        row_pass(half, False)
    lane_sums(0, 0, part)
    rows_start(0, 16)
    both = rows_end(0, 16)
    to_column(rcol, 1.0 / (both[0:8] * TOTAL_ROWS))
    for half in range(2):
        col_pass(1, half)
        columns_start(1, half)
    log_total = jnp.log(both[8:16])
    to_column(ltot, (log_total - math.log(GRAD_SCALE)) * LOG2E)
    for half in range(2):
        columns_end(1, half)
        row_pass(half, False)
    lane_sums(1, 0, part)
    rows_start(1, 8)
    row_sum = rows_end(1, 8)
    to_column(rcol, 1.0 / (row_sum * TOTAL_ROWS))
    for half in range(2):
        col_pass(2, half)
        columns_start(2, half)
    for half in range(2):
        columns_end(2, half)
        row_pass(half, True)
    lane_sums(2, 0, part)
    lane_sums(2, 8, part2)
    rows_start(2, 16)
    both = rows_end(2, 16)
    row_sum = both[0:8]
    row_scale = 1.0 / (row_sum * TOTAL_ROWS)
    to_column(rcol, row_scale * (TOTAL_ROWS * GRAD_SCALE))
    target_sum = row_sum * (row_scale * TOTAL_ROWS)
    target_logits = both[8:16] * (row_scale * (TOTAL_ROWS / LOG2E))
    lossrow[...] = log_total * target_sum - target_logits

    ahead = {0: (chip_at(0, 1), chip_at(0, 3), x), 1: (chip_at(1, 0), chip_at(3, 0), y)}
    feat[...] = jnp.zeros_like(feat)

    def make_grad(j, slot):
        for rb in range(ROWS // STEP):
            at = slice(rb * STEP, (rb + 1) * STEP)
            scale = rcol[at, :]
            shift = ltot[at, :]
            for t in range(2 * CH // LANES):
                tile = j * (2 * CH // LANES) + t
                cut = pl.ds(aligned(tile * LANES, LANES), LANES)
                probs = jnp.exp2(l_ref[at, cut] - shift)
                target = e_ref[at, cut] * cscale[pl.ds(tile, 1), :] * scale
                grad[slot, at, t * LANES:(t + 1) * LANES] = (probs - target).astype(BF16)

    def products(j, slot):
        for kind in range(2):
            q = 2 * j + kind
            value = jnp.dot(sut[kind], grad[slot, :, kind * CH:(kind + 1) * CH], preferred_element_type=F32)
            pg[q] = value
            for t in range(CH // LANES):
                cut = pl.ds(aligned(q * CH + t * LANES, LANES), LANES)
                inner = jnp.zeros((16, LANES), F32)
                for yy in range(NY):
                    for xx in range(NX):
                        at = (yy * NX + xx) * 16
                        to = (xx * NY + yy) * 16 if kind == 0 else at
                        inner = inner + (
                            sw[at:at + 16, cut].astype(F32) * value[to:to + 16, t * LANES:(t + 1) * LANES]
                        )
                ipart[q * (CH // 256) + t // 2, t % 2:t % 2 + 1, :] = jnp.sum(inner, axis=0, keepdims=True)
        cols = pl.ds(aligned(j * 2 * CH, 2 * CH), 2 * CH)
        feat[...] += lax.dot_general(
            grad[slot], sp[:, cols], (((1,), (1,)), ((), ())), preferred_element_type=F32
        )

    def first_opposite(j):
        for kind in range(2):
            q = 2 * j + kind
            plus, minus, a = ahead[kind]
            opposite = lax.rem(a + 2, 4) * 64
            send(pg.at[q, pl.ds(aligned(opposite, 32), 32)], r1.at[q, 0], rs_send.at[q, 0], rs_recv.at[q, 0], plus)
            send(pg.at[q, pl.ds(aligned(opposite + 32, 32), 32)], r1.at[q, 1], rs_send.at[q, 0], rs_recv.at[q, 1], minus)

    def first_direct(j):
        for kind in range(2):
            q = 2 * j + kind
            plus, minus, a = ahead[kind]
            ap, am = lax.rem(a + 1, 4) * 64, lax.rem(a + 3, 4) * 64
            send(pg.at[q, pl.ds(aligned(ap + 32, 32), 32)], r2.at[q, 0, pl.ds(32, 32)], rs_send.at[q, 0], rs_recv.at[q, 2], plus)
            send(pg.at[q, pl.ds(aligned(am, 32), 32)], r2.at[q, 1, pl.ds(0, 32)], rs_send.at[q, 0], rs_recv.at[q, 2], minus)

    def first_forward(j, whole):
        for kind in range(2):
            q = 2 * j + kind
            plus, minus, a = ahead[kind]
            ap = aligned(lax.rem(a + 1, 4) * 64, 64)
            am = aligned(lax.rem(a + 3, 4) * 64, 64)
            low, high = pl.ds(ap, 32), pl.ds(aligned(am + 32, 32), 32)
            await_bytes(r1.at[q, 0], rs_recv.at[q, 0])
            pg[q, low, :] = pg[q, low, :] + r1[q, 0]
            if whole:
                send(pg.at[q, pl.ds(ap, 64)], r2.at[q, 0], rs_send.at[q, 0], rs_recv.at[q, 2], plus)
            else:
                send(pg.at[q, low], r2.at[q, 0, pl.ds(0, 32)], rs_send.at[q, 0], rs_recv.at[q, 2], plus)
            await_bytes(r1.at[q, 1], rs_recv.at[q, 1])
            pg[q, high, :] = pg[q, high, :] + r1[q, 1]
            if whole:
                send(pg.at[q, pl.ds(am, 64)], r2.at[q, 1], rs_send.at[q, 0], rs_recv.at[q, 2], minus)
            else:
                send(pg.at[q, high], r2.at[q, 1, pl.ds(32, 32)], rs_send.at[q, 0], rs_recv.at[q, 2], minus)

    def second_start(j):
        for kind in range(2):
            q = 2 * j + kind
            a = ahead[kind][2]
            plus, minus, b = ahead[1 - kind]
            await_bytes(r2.at[q], rs_recv.at[q, 2])
            second[q] = pg[q, pl.ds(aligned(a * 64, 64), 64), :] + r2[q, 0] + r2[q, 1]
            opposite = lax.rem(b + 2, 4) * 16
            bp, bm = lax.rem(b + 1, 4) * 16, lax.rem(b + 3, 4) * 16
            send(second.at[q, pl.ds(aligned(opposite, 8), 8)], r3.at[q, 0], rs_send.at[q, 1], rs_recv.at[q, 3], plus)
            send(second.at[q, pl.ds(aligned(opposite + 8, 8), 8)], r3.at[q, 1], rs_send.at[q, 1], rs_recv.at[q, 4], minus)
            send(second.at[q, pl.ds(aligned(bp + 8, 8), 8)], r4.at[q, 0, pl.ds(8, 8)], rs_send.at[q, 1], rs_recv.at[q, 5], plus)
            send(second.at[q, pl.ds(aligned(bm, 8), 8)], r4.at[q, 1, pl.ds(0, 8)], rs_send.at[q, 1], rs_recv.at[q, 5], minus)

    def second_forward(j):
        for kind in range(2):
            q = 2 * j + kind
            plus, minus, b = ahead[1 - kind]
            bp = aligned(lax.rem(b + 1, 4) * 16, 8)
            bm = aligned(lax.rem(b + 3, 4) * 16 + 8, 8)
            await_bytes(r3.at[q, 0], rs_recv.at[q, 3])
            second[q, pl.ds(bp, 8), :] = second[q, pl.ds(bp, 8), :] + r3[q, 0]
            send(second.at[q, pl.ds(bp, 8)], r4.at[q, 0, pl.ds(0, 8)], rs_send.at[q, 1], rs_recv.at[q, 5], plus)
            await_bytes(r3.at[q, 1], rs_recv.at[q, 4])
            second[q, pl.ds(bm, 8), :] = second[q, pl.ds(bm, 8), :] + r3[q, 1]
            send(second.at[q, pl.ds(bm, 8)], r4.at[q, 1, pl.ds(8, 8)], rs_send.at[q, 1], rs_recv.at[q, 5], minus)

    chip_rows = pl.ds(aligned(chip * 16, 16), 16)

    def finish(j):
        for kind in range(2):
            q = 2 * j + kind
            b = ahead[1 - kind][2]
            await_bytes(r4.at[q], rs_recv.at[q, 5])
            total = second[q, pl.ds(aligned(b * 16, 16), 16), :] + r4[q, 0] + r4[q, 1]
            for t in range(CH // LANES):
                tile = q * (CH // LANES) + t
                cut = slice(tile * LANES, (tile + 1) * LANES)
                inverse = cinv[tile:tile + 1, :]
                inner = inner_all[tile // 2, tile % 2:tile % 2 + 1, :] * (inverse * inverse * inverse)
                value = inverse * total[:, t * LANES:(t + 1) * LANES] - sw[chip_rows, cut].astype(F32) * inner
                gwfull[k, 0, :, cut] = value[0:8]
                gwfull[k, 1, :, cut] = value[8:16]
        cols = pl.ds(j * 2 * CH, 2 * CH)
        send(gwfull.at[k, other, :, cols], gwfull.at[k, other, :, cols], gw_send.at[j], gw_recv.at[j], sibling)
        leaving.append((gwfull.at[k, other, :, cols], gw_send.at[j]))

    def inner_start():
        for slot, (dy, dx) in enumerate(COL_PEERS):
            if slot:
                to = lax.rem(y + dy, NY) * NX + lax.rem(x + dx, NX)
                send(ipart.at[to], irecv.at[slot], inner_send.at[0], inner_recv.at[0], chip_at(dy, dx))
        leaving.append((irecv.at[pl.ds(1, CHIPS - 1)], inner_send.at[0]))

    def inner_middle():
        await_bytes(irecv.at[pl.ds(1, CHIPS - 1)], inner_recv.at[0])
        total = ipart[chip]
        for slot in range(1, CHIPS):
            total = total + irecv[slot]
        inner_all[chip] = total
        for dy, dx in COL_PEERS[1:]:
            send(inner_all.at[chip], inner_all.at[chip], inner_send.at[1], inner_recv.at[1], chip_at(dy, dx))
        leaving.append((irecv.at[pl.ds(1, CHIPS - 1)], inner_send.at[1]))

    def inner_end():
        await_bytes(irecv.at[pl.ds(1, CHIPS - 1)], inner_recv.at[1])

    def feature_sibling():
        send(feat.at[half_rows(other)], fsib, feat_send.at[0], feat_recv.at[0], sibling)
        leaving.append((fsib, feat_send.at[0]))

    def share(where, half):
        return aligned(where * ZROWS + half * ZHALF, ZHALF)

    def feature_scatter():
        await_bytes(fsib, feat_recv.at[0])
        fsib[...] = feat[half_rows(k), :] + fsib[...]
        for half in range(2):
            for dz in range(1, NZ):
                to = lax.rem(z + dz, NZ)
                send(
                    fsib.at[pl.ds(share(to, half), ZHALF)], fz.at[half, dz],
                    feat_send.at[1 + half], feat_recv.at[1 + half], row_at(dz, 0),
                )
            leaving.append((fz.at[half, pl.ds(1, NZ - 1)], feat_send.at[1 + half]))

    def feature_gather(half):
        await_bytes(fz.at[half, pl.ds(1, NZ - 1)], feat_recv.at[1 + half])
        rows = pl.ds(share(z, half), ZHALF)
        feature = fsib[rows, :]
        for dz in range(1, NZ):
            feature = feature + fz[half, dz]
        rows_wide = srow[rows, :]
        inverse = rinv[rows, 0:1]
        rg[rows, :] = inverse * feature - rows_wide * (inverse * inverse * inverse) * jnp.sum(
            rows_wide * feature, axis=1, keepdims=True
        )
        for dz in range(1, NZ):
            send(rg.at[rows], rg.at[rows], feat_send.at[3 + half], feat_recv.at[3 + half], row_at(dz, 0))
        leaving.append((fz.at[half, pl.ds(1, NZ - 1)], feat_send.at[3 + half]))

    def feature_end(half):
        await_bytes(fz.at[half, pl.ds(1, NZ - 1)], feat_recv.at[3 + half])

    make_grad(0, 0)
    products(0, 0)
    first_opposite(0)
    first_direct(0)
    make_grad(1, 1)

    def gradient(j, carry):
        slot = lax.rem(j, 2)
        products(j, slot)
        make_grad(j + 1, 1 - slot)
        first_opposite(j)

        @pl.when(j < EARLY)
        def direct():
            first_direct(j)

        @pl.when(j >= LAG)
        def forward():
            first_forward(j - LAG, False)

        return carry

    lax.fori_loop(1, PAIRS - 1, gradient, 0)
    products(PAIRS - 1, (PAIRS - 1) % 2)
    feature_sibling()
    first_opposite(PAIRS - 1)
    inner_start()
    for j in range(PAIRS - 1 - LAG, PAIRS):
        first_forward(j, j >= EARLY)
        if j == PAIRS - 1 - LAG:
            feature_scatter()
    for j in range(PAIRS):
        second_start(j)
        if j == PAIRS // 2:
            inner_middle()
        if j == PAIRS - 2:
            feature_gather(0)
        if j >= DELAY:
            second_forward(j - DELAY)
    feature_gather(1)
    inner_end()
    for j in range(PAIRS - DELAY, PAIRS):
        second_forward(j)
        finish(j - PAIRS + DELAY)
    for j in range(DELAY, PAIRS):
        finish(j)
    loss_ref[...] = jnp.where(k == 0, lossrow[0:3, :], lossrow[3:6, :])
    feature_end(0)
    feature_end(1)
    rg_ref[...] = rg[...]
    for j in range(PAIRS):
        await_bytes(gwfull.at[other, k, :, pl.ds(j * 2 * CH, 2 * CH)], gw_recv.at[j])
    for core in range(NK):
        gw_ref[core] = gwfull[core, k]

    for ref, sem in leaving:
        await_bytes(ref, sem)

    def sent(q, carry):
        await_bytes(pg.at[q, pl.ds(0, 192)], rs_send.at[q, 0])
        await_bytes(second.at[q, pl.ds(0, 48)], rs_send.at[q, 1])
        return carry

    lax.fori_loop(0, PARTS, sent, 0)


def finish_kernel(midx, loss_part, gw_part, rg, loss_ref, gw_ref, gp_ref):
    for row in range(OWN // LANES):
        loss_ref[row * LANES:(row + 1) * LANES] = loss_part[row, :]
    for core in range(NK):
        gw_ref[:, core * COLS:(core + 1) * COLS] = gw_part[core]
    index = midx[...].reshape(1, OWN)
    patch_id = lax.broadcasted_iota(jnp.int32, (PATCH, OWN), 0)
    scatter = jnp.where(patch_id == index, 1.0, 0.0).astype(BF16)
    value = rg[...]
    high = value.astype(BF16)
    value = value - high.astype(F32)
    middle = value.astype(BF16)
    low = (value - middle.astype(F32)).astype(BF16)
    gp_ref[...] = (
        jnp.dot(scatter, low, preferred_element_type=F32)
        + jnp.dot(scatter, middle, preferred_element_type=F32)
        + jnp.dot(scatter, high, preferred_element_type=F32)
    )


def shards(teacher_patches, student_patches, mask_index, teacher_weight, student_weight):
    vmem = pl.BlockSpec(memory_space=pltpu.VMEM)
    hbm = pl.BlockSpec(memory_space=pl.ANY)
    dma = pltpu.SemaphoreType.DMA
    scratch = [
        pltpu.VMEM((PATCH, WIDTH), BF16),
        pltpu.VMEM((PATCH, WIDTH), BF16),
        pltpu.VMEM((WIDTH, COLS), BF16),
        pltpu.VMEM((WIDTH, COLS), BF16),
        pltpu.VMEM((WIDTH, COLS), BF16),
        pltpu.VMEM((WIDTH, COLS), BF16),
        pltpu.VMEM((TILES, LANES), F32),
        pltpu.VMEM((2, NK, OWN, WIDTH), F32),
        pltpu.VMEM((ROWS, WIDTH), BF16),
        pltpu.VMEM((ROWS, WIDTH), BF16),
        pltpu.VMEM((2, WIDTH, ROWS), BF16),
        pltpu.VMEM((OWN, WIDTH), F32),
        pltpu.VMEM((OWN, LANES), F32),
        pltpu.VMEM((ROWS, COLS), F32),
        pltpu.VMEM((ROWS, COLS), F32),
        pltpu.VMEM((ROWS, LANES), F32),
        pltpu.VMEM((ROWS, LANES), F32),
        pltpu.VMEM((3, TILES, LANES), F32),
        pltpu.VMEM((3, CHIPS, TILES, LANES), F32),
        pltpu.VMEM((TILES, LANES), F32),
        pltpu.VMEM((3, 16, LANES), F32),
        pltpu.VMEM((3, NZ * NK, 16, LANES), F32),
        pltpu.VMEM((ROWS, LANES), F32),
        pltpu.VMEM((ROWS, LANES), F32),
        pltpu.VMEM((2, ROWS, 2 * CH), BF16),
        pltpu.VMEM((PARTS, WIDTH, CH), F32),
        pltpu.VMEM((PARTS, 2, 32, CH), F32),
        pltpu.VMEM((PARTS, 2, 64, CH), F32),
        pltpu.VMEM((PARTS, 2, 8, CH), F32),
        pltpu.VMEM((PARTS, 2, 16, CH), F32),
        pltpu.VMEM((PARTS, 64, CH), F32),
        pltpu.VMEM((ROWS, WIDTH), F32),
        pltpu.VMEM((OWN, WIDTH), F32),
        pltpu.VMEM((2, NZ, ZHALF, WIDTH), F32),
        pltpu.VMEM((OWN, WIDTH), F32),
        pltpu.VMEM((NK, NK, 8, COLS), F32),
        pltpu.VMEM((8, LANES), F32),
        pltpu.VMEM((CHIPS, 2, LANES), F32),
        pltpu.VMEM((CHIPS, 2, LANES), F32),
        pltpu.VMEM((CHIPS, 2, LANES), F32),
        dma((4,)),
        dma((2,)),
        dma((2,)),
        dma((3, 2)),
        dma((3, 2)),
        dma((3,)),
        dma((3,)),
        dma((PARTS, 2)),
        dma((PARTS, 6)),
        dma((5,)),
        dma((5,)),
        dma((PAIRS,)),
        dma((PAIRS,)),
        dma((2,)),
        dma((2,)),
    ]
    loss_part, gw_part, row_grad = pl.pallas_call(
        kernel,
        out_shape=(
            jax.ShapeDtypeStruct((OWN // LANES, LANES), F32),
            jax.ShapeDtypeStruct((NK, WIDTH // DP, COLS), F32),
            jax.ShapeDtypeStruct((OWN, WIDTH), F32),
        ),
        in_specs=[hbm, hbm, vmem, hbm, hbm],
        out_specs=(vmem, vmem, vmem),
        scratch_shapes=scratch,
        compiler_params=pltpu.CompilerParams(
            collective_id=0, has_side_effects=True, vmem_limit_bytes=60 * 1024 * 1024
        ),
    )(teacher_patches, student_patches, mask_index, teacher_weight, student_weight)
    return pl.pallas_call(
        finish_kernel,
        out_shape=(
            jax.ShapeDtypeStruct((OWN,), F32),
            jax.ShapeDtypeStruct((WIDTH // DP, NK * COLS), F32),
            jax.ShapeDtypeStruct((PATCH, WIDTH), F32),
        ),
        in_specs=[vmem] * 4,
        out_specs=(vmem, vmem, vmem),
    )(mask_index, loss_part, gw_part, row_grad)


def solution(mesh):
    placed = (P("dp", None), P("dp", None), P("dp"), P(None, "proto"), P(None, "proto"))
    return jax.shard_map(
        shards,
        mesh=mesh,
        in_specs=placed,
        out_specs=(P("dp"), P("dp", "proto"), P("dp", None)),
        check_vma=False,
    )
```

```python
import math

import jax
import jax.numpy as jnp
from jax import lax
from jax.experimental import pallas as pl
from jax.experimental.pallas import tpu as pltpu
from jax.sharding import PartitionSpec as P

MESH = pl.DeviceIdType.MESH
F32 = jnp.float32
BF16 = jnp.bfloat16

EPS = 1e-06
TEACHER_TEMP = 0.07
STUDENT_TEMP = 0.1
LOG2E = 1.0 / math.log(2.0)

NY, NX, NK, NZ = 4, 4, 2, 8
DP = NY * NX * NK
CHIPS = NY * NX
OWN = 384
ROWS = NK * OWN
WIDTH = 256
PATCH = 768
COLS = 4096
LANES = 128
CH = 512
PARTS = COLS // CH
TOTAL_ROWS = OWN * DP
TOTAL_PROTOS = COLS * NK * NZ
ZROWS = OWN // NZ
GRAD_SCALE = 1.0 / (TOTAL_ROWS * STUDENT_TEMP)
COL_PEERS = [(dy, dx) for dy in range(NY) for dx in range(NX)]
ROW_PEERS = [(dz, dk) for dz in range(NZ) for dk in range(NK)]
PAIRS = PARTS // 2
TILES = COLS // LANES
SPLIT = 2
PIECE = TILES // SPLIT
RB = 128
STEP = 64
ZHALF = ZROWS // 2
LAG = 2
EARLY = PAIRS // 2


def farthest_first(peers, sizes):
    return sorted(enumerate(peers), key=lambda at: -sum(min(d, n - d) for d, n in zip(at[1], sizes)))[:-1]


COL_ORDER = farthest_first(COL_PEERS, (NY, NX))
ROW_ORDER = farthest_first(ROW_PEERS, (NZ, NK))
Z_ORDER = [4, 3, 5, 2, 6, 1, 7]


def aligned(value, unit):
    return pl.multiple_of(value, unit)


def kernel(
    tpat_hbm, spat_hbm, midx, tw_hbm, sw_hbm,
    loss_ref, gw_ref, rg_ref,
    tpat, spat, tw, sw, tp, sp, cinv, units, tu, su, sut, srow, rinv,
    e_ref, l_ref, part, part2, csend, crecv, cscale, rsend, rrecv, rcol, ltot,
    grad, pg, r1, r2, r4, second, feat, fsib, fz, rg, gwfull, lossrow,
    isend, irecv,
    load_sem, unit_send, unit_recv, col_send, col_recv, row_send, row_recv,
    rs_send, rs_recv, feat_send, feat_recv, gw_send, gw_recv, inner_send, inner_recv,
):
    dp = lax.axis_index("dp")
    z = lax.axis_index("proto")
    k = lax.rem(dp, NK)
    chip = lax.div(dp, NK)
    x = lax.rem(chip, NX)
    y = lax.div(chip, NX)
    other = lax.rem(k + 1, NK)

    def device(yy, xx, kk, zz):
        return ((yy * NX + xx) * NK + kk, zz)

    def chip_at(dy, dx):
        return device(lax.rem(y + dy, NY), lax.rem(x + dx, NX), k, z)

    def row_at(dz, dk):
        return device(y, x, lax.rem(k + dk, NK), lax.rem(z + dz, NZ))

    sibling = row_at(0, 1)

    def send(src, dst, send_sem, recv_sem, where):
        copy = pltpu.make_async_remote_copy(
            src_ref=src, dst_ref=dst, send_sem=send_sem, recv_sem=recv_sem,
            device_id=where, device_id_type=MESH,
        )
        copy.start()

    def await_bytes(ref, sem):
        pltpu.make_async_copy(ref, ref, sem).wait()

    leaving = []

    loads = []
    mine = pl.ds(aligned(k * COLS, COLS), COLS)
    for turn, (src, dst) in enumerate(
        ((tpat_hbm, tpat), (tw_hbm.at[:, mine], tw), (spat_hbm, spat), (sw_hbm.at[:, mine], sw))
    ):
        loads.append(pltpu.make_async_copy(src, dst, load_sem.at[turn]))
        loads[-1].start()

    barrier = pltpu.get_barrier_semaphore()
    for _, (dz, dk) in ROW_ORDER:
        pl.semaphore_signal(barrier, inc=1, device_id=row_at(dz, dk), device_id_type=MESH)
    for _, (dy, dx) in COL_ORDER:
        pl.semaphore_signal(barrier, inc=1, device_id=chip_at(dy, dx), device_id_type=MESH)

    def half_rows(core):
        return pl.ds(aligned(core * OWN, LANES), OWN)

    index = midx[...].reshape(1, OWN)
    index_col = jnp.transpose(jnp.broadcast_to(index.astype(F32), (LANES, OWN)))
    lane = lax.broadcasted_iota(jnp.int32, (OWN, LANES), 1).astype(F32)
    onehot = jnp.concatenate(
        [jnp.where(index_col == lane + float(t * LANES), 1.0, 0.0) for t in range(PATCH // LANES)], axis=1
    ).astype(BF16)

    def unit_rows(side, patches, ref):
        rows = jnp.dot(onehot, patches[...], preferred_element_type=F32)
        inverse = lax.rsqrt(jnp.sum(rows * rows, axis=1, keepdims=True) + EPS)
        unit = (rows * inverse).astype(BF16)
        ref[half_rows(k), :] = unit
        units[side, k] = unit.astype(F32)
        return rows, inverse

    loads[0].wait()
    unit_rows(0, tpat, tu)
    loads[2].wait()
    srow_value, sinv = unit_rows(1, spat, su)
    srow[...] = srow_value
    rinv[...] = jnp.broadcast_to(sinv, (OWN, LANES))

    def teacher_columns(j, carry):
        cols = pl.ds(aligned(j * CH, CH), CH)
        wide = tw[:, cols].astype(F32)
        inverse = lax.rsqrt(jnp.sum(wide * wide, axis=0, keepdims=True) + EPS)
        tp[:, cols] = (wide * inverse).astype(BF16)
        return carry

    def student_columns(j, carry):
        cols = pl.ds(aligned(j * CH, CH), CH)
        wide = sw[:, cols].astype(F32)
        inverse = lax.rsqrt(jnp.sum(wide * wide, axis=0, keepdims=True) + EPS)
        for t in range(CH // LANES):
            cinv[pl.ds(j * (CH // LANES) + t, 1), :] = inverse[:, t * LANES:(t + 1) * LANES]
        sp[:, cols] = (wide * inverse).astype(BF16)
        return carry

    def teacher_exp(core, first, last, add):
        def body(j, carry):
            cols = pl.ds(aligned(j * CH, CH), CH)
            total = jnp.zeros((1, CH), F32)
            for rb in range(OWN // RB):
                at = pl.ds(aligned(core * OWN + rb * RB, RB), RB)
                value = jnp.exp2(
                    jnp.dot(tu[at, :], tp[:, cols], preferred_element_type=F32) * (LOG2E / TEACHER_TEMP)
                )
                e_ref[at, cols] = value
                total = total + jnp.sum(value, axis=0, keepdims=True)
            for t in range(CH // LANES):
                row = pl.ds(j * (CH // LANES) + t, 1)
                piece = total[:, t * LANES:(t + 1) * LANES]
                csend[0, row, :] = csend[0, row, :] + piece if add else piece
            return carry

        lax.fori_loop(first, last, body, 0)

    def student_logits(core):
        def body(j, carry):
            cols = pl.ds(aligned(j * CH, CH), CH)
            for rb in range(OWN // RB):
                at = pl.ds(aligned(core * OWN + rb * RB, RB), RB)
                value = jnp.dot(su[at, :], sp[:, cols], preferred_element_type=F32) * (LOG2E / STUDENT_TEMP)
                l_ref[at, cols] = value
                power = jnp.exp2(value)
                total = part2[at, :]
                for t in range(CH // LANES):
                    total = total + power[:, t * LANES:(t + 1) * LANES]
                part2[at, :] = total
            return carry

        lax.fori_loop(0, PARTS, body, 0)

    def columns_start(turn, piece):
        cut = pl.ds(piece * PIECE, PIECE)
        for slot, (dy, dx) in COL_ORDER:
            send(
                csend.at[turn, cut], crecv.at[turn, slot, cut],
                col_send.at[turn, piece], col_recv.at[turn, piece], chip_at(dy, dx),
            )
        leaving.append((crecv.at[turn, pl.ds(1, CHIPS - 1), cut], col_send.at[turn, piece]))

    def columns_end(turn, piece):
        cut = pl.ds(piece * PIECE, PIECE)
        await_bytes(crecv.at[turn, pl.ds(1, CHIPS - 1), cut], col_recv.at[turn, piece])
        total = csend[turn, cut, :]
        for slot in range(1, CHIPS):
            total = total + crecv[turn, slot, cut, :]
        cscale[cut, :] = 1.0 / (total * TOTAL_PROTOS)

    def rows_start(turn):
        for slot, (dz, dk) in ROW_ORDER:
            send(rsend.at[turn], rrecv.at[turn, slot], row_send.at[turn], row_recv.at[turn], row_at(dz, dk))
        leaving.append((rrecv.at[turn, pl.ds(1, NZ * NK - 1)], row_send.at[turn]))

    def rows_end(turn):
        await_bytes(rrecv.at[turn, pl.ds(1, NZ * NK - 1)], row_recv.at[turn])
        total = rsend[turn]
        for slot in range(1, NZ * NK):
            total = total + rrecv[turn, slot]
        return total

    def to_column(ref, rows):
        for b in range(ROWS // LANES):
            ref[b * LANES:(b + 1) * LANES, :] = jnp.transpose(jnp.broadcast_to(rows[b:b + 1, :], (LANES, LANES)))

    def lane_sums(turn, ref):
        for b in range(ROWS // LANES):
            rsend[turn, b:b + 1, :] = jnp.sum(
                jnp.transpose(ref[b * LANES:(b + 1) * LANES, :]), axis=0, keepdims=True
            )

    def row_pass(piece):
        def body(rb, carry):
            at = pl.ds(aligned(rb * STEP, STEP), STEP)
            total = part[at, :] if piece else jnp.zeros((STEP, LANES), F32)
            for t in range(piece * PIECE, (piece + 1) * PIECE):
                cut = slice(t * LANES, (t + 1) * LANES)
                total = total + e_ref[at, cut] * cscale[t:t + 1, :]
            part[at, :] = total
            return carry

        lax.fori_loop(0, ROWS // STEP, body, 0)

    def cross_pass():
        def body(rb, carry):
            at = pl.ds(aligned(rb * STEP, STEP), STEP)
            total = jnp.zeros((STEP, LANES), F32)
            for t in range(TILES):
                cut = slice(t * LANES, (t + 1) * LANES)
                total = total + e_ref[at, cut] * cscale[t:t + 1, :] * l_ref[at, cut]
            part2[at, :] = total
            return carry

        lax.fori_loop(0, ROWS // STEP, body, 0)

    def col_pass(turn, piece):
        def body(rb, totals):
            at = pl.ds(aligned(rb * STEP, STEP), STEP)
            scale = rcol[at, :]
            out = []
            for t in range(PIECE):
                cut = slice((piece * PIECE + t) * LANES, (piece * PIECE + t + 1) * LANES)
                value = e_ref[at, cut] * scale
                out.append(totals[t] + jnp.sum(value.reshape(STEP // 8, 8, LANES), axis=0))
            return tuple(out)

        totals = lax.fori_loop(0, ROWS // STEP, body, tuple(jnp.zeros((8, LANES), F32) for _ in range(PIECE)))
        for t in range(PIECE):
            row = piece * PIECE + t
            csend[turn, row:row + 1, :] = jnp.sum(totals[t], axis=0, keepdims=True)

    loads[1].wait()
    lax.fori_loop(0, PARTS, teacher_columns, 0)
    teacher_exp(k, 0, PARTS, False)
    part2[...] = jnp.zeros_like(part2)
    rsend[...] = jnp.zeros_like(rsend)

    pl.semaphore_wait(barrier, CHIPS - 1 + NZ * NK - 1)
    for side in range(2):
        send(units.at[side, k], units.at[side, k], unit_send.at[side], unit_recv.at[side], sibling)
        leaving.append((units.at[side, k], unit_send.at[side]))
    loads[3].wait()
    lax.fori_loop(0, PARTS, student_columns, 0)
    await_bytes(units.at[0, other], unit_recv.at[0])
    tu[half_rows(other), :] = units[0, other].astype(BF16)
    for piece in range(SPLIT):
        teacher_exp(other, piece * PARTS // SPLIT, (piece + 1) * PARTS // SPLIT, True)
        columns_start(0, piece)
    await_bytes(units.at[1, other], unit_recv.at[1])
    su[half_rows(other), :] = units[1, other].astype(BF16)
    student_logits(k)
    student_logits(other)
    for piece in range(SPLIT):
        columns_end(0, piece)
        row_pass(piece)
    lane_sums(0, part)
    rows_start(0)
    lane_sums(3, part2)
    rows_start(3)
    for core in range(NK):
        sut[1, :, core * OWN:(core + 1) * OWN] = jnp.transpose(units[1, core]).astype(BF16)
    for xx in range(NX):
        for yy in range(NY):
            to, at = (xx * NY + yy) * 16, (yy * NX + xx) * 16
            sut[0, to:to + 16, :] = sut[1, at:at + 16, :]
    to_column(rcol, 1.0 / (rows_end(0) * TOTAL_ROWS))
    for piece in range(SPLIT):
        col_pass(1, piece)
        columns_start(1, piece)
    log_total = jnp.log(rows_end(3))
    to_column(ltot, (log_total - math.log(GRAD_SCALE)) * LOG2E)
    for piece in range(SPLIT):
        columns_end(1, piece)
        row_pass(piece)
    lane_sums(1, part)
    rows_start(1)
    to_column(rcol, 1.0 / (rows_end(1) * TOTAL_ROWS))
    for piece in range(SPLIT):
        col_pass(2, piece)
        columns_start(2, piece)
    for piece in range(SPLIT):
        columns_end(2, piece)
        row_pass(piece)
    lane_sums(2, part)
    rows_start(2)
    cross_pass()
    lane_sums(4, part2)
    rows_start(4)
    row_sum = rows_end(2)
    row_scale = 1.0 / (row_sum * TOTAL_ROWS)
    to_column(rcol, row_scale * (TOTAL_ROWS * GRAD_SCALE))

    ahead = {0: (chip_at(0, 1), chip_at(0, 3), x), 1: (chip_at(1, 0), chip_at(3, 0), y)}
    across = {0: chip_at(0, 2), 1: chip_at(2, 0)}
    feat[...] = jnp.zeros_like(feat)

    def make_grad(j, slot):
        for rb in range(ROWS // STEP):
            at = slice(rb * STEP, (rb + 1) * STEP)
            scale = rcol[at, :]
            shift = ltot[at, :]
            for t in range(2 * CH // LANES):
                tile = j * (2 * CH // LANES) + t
                cut = pl.ds(aligned(tile * LANES, LANES), LANES)
                probs = jnp.exp2(l_ref[at, cut] - shift)
                target = e_ref[at, cut] * cscale[pl.ds(tile, 1), :] * scale
                grad[slot, at, t * LANES:(t + 1) * LANES] = (probs - target).astype(BF16)

    def products(j, slot):
        for kind in range(2):
            q = 2 * j + kind
            value = jnp.dot(sut[kind], grad[slot, :, kind * CH:(kind + 1) * CH], preferred_element_type=F32)
            pg[q] = value
            for t in range(CH // LANES):
                cut = pl.ds(aligned(q * CH + t * LANES, LANES), LANES)
                inner = jnp.zeros((16, LANES), F32)
                for yy in range(NY):
                    for xx in range(NX):
                        at = (yy * NX + xx) * 16
                        to = (xx * NY + yy) * 16 if kind == 0 else at
                        inner = inner + (
                            sw[at:at + 16, cut].astype(F32) * value[to:to + 16, t * LANES:(t + 1) * LANES]
                        )
                isend[0, pl.ds(q * (CH // LANES) + t, 1), :] = jnp.sum(inner, axis=0, keepdims=True)
        cols = pl.ds(aligned(j * 2 * CH, 2 * CH), 2 * CH)
        feat[...] += lax.dot_general(
            grad[slot], sp[:, cols], (((1,), (1,)), ((), ())), preferred_element_type=F32
        )

    def first_opposite(j):
        for kind in range(2):
            q = 2 * j + kind
            plus, minus, a = ahead[kind]
            opposite = lax.rem(a + 2, 4) * 64
            send(pg.at[q, pl.ds(aligned(opposite, 32), 32)], r1.at[q, 0], rs_send.at[q, 0], rs_recv.at[q, 0], plus)
            send(pg.at[q, pl.ds(aligned(opposite + 32, 32), 32)], r1.at[q, 1], rs_send.at[q, 0], rs_recv.at[q, 1], minus)

    def first_direct(j):
        for kind in range(2):
            q = 2 * j + kind
            plus, minus, a = ahead[kind]
            ap, am = lax.rem(a + 1, 4) * 64, lax.rem(a + 3, 4) * 64
            send(pg.at[q, pl.ds(aligned(ap + 32, 32), 32)], r2.at[q, 0, pl.ds(32, 32)], rs_send.at[q, 0], rs_recv.at[q, 2], plus)
            send(pg.at[q, pl.ds(aligned(am, 32), 32)], r2.at[q, 1, pl.ds(0, 32)], rs_send.at[q, 0], rs_recv.at[q, 2], minus)

    def first_forward(j, whole):
        for kind in range(2):
            q = 2 * j + kind
            plus, minus, a = ahead[kind]
            ap = aligned(lax.rem(a + 1, 4) * 64, 64)
            am = aligned(lax.rem(a + 3, 4) * 64, 64)
            low, high = pl.ds(ap, 32), pl.ds(aligned(am + 32, 32), 32)
            await_bytes(r1.at[q, 0], rs_recv.at[q, 0])
            pg[q, low, :] = pg[q, low, :] + r1[q, 0]
            if whole:
                send(pg.at[q, pl.ds(ap, 64)], r2.at[q, 0], rs_send.at[q, 0], rs_recv.at[q, 2], plus)
            else:
                send(pg.at[q, low], r2.at[q, 0, pl.ds(0, 32)], rs_send.at[q, 0], rs_recv.at[q, 2], plus)
            await_bytes(r1.at[q, 1], rs_recv.at[q, 1])
            pg[q, high, :] = pg[q, high, :] + r1[q, 1]
            if whole:
                send(pg.at[q, pl.ds(am, 64)], r2.at[q, 1], rs_send.at[q, 0], rs_recv.at[q, 2], minus)
            else:
                send(pg.at[q, high], r2.at[q, 1, pl.ds(32, 32)], rs_send.at[q, 0], rs_recv.at[q, 2], minus)

    def second_start(j):
        for kind in range(2):
            q = 2 * j + kind
            a = ahead[kind][2]
            plus, minus, b = ahead[1 - kind]
            await_bytes(r2.at[q], rs_recv.at[q, 2])
            second[q] = pg[q, pl.ds(aligned(a * 64, 64), 64), :] + r2[q, 0] + r2[q, 1]
            for slot, where in ((2, across[1 - kind]), (0, plus), (1, minus)):
                block = pl.ds(aligned(lax.rem(b + (1, 3, 2)[slot], 4) * 16, 16), 16)
                send(second.at[q, block], r4.at[q, slot], rs_send.at[q, 1], rs_recv.at[q, 3], where)

    chip_rows = pl.ds(aligned(chip * 16, 16), 16)

    def finish(j):
        if j == 0:
            inner_end(1)
        for kind in range(2):
            q = 2 * j + kind
            b = ahead[1 - kind][2]
            await_bytes(r4.at[q], rs_recv.at[q, 3])
            total = second[q, pl.ds(aligned(b * 16, 16), 16), :] + r4[q, 0] + r4[q, 1] + r4[q, 2]
            for t in range(CH // LANES):
                tile = q * (CH // LANES) + t
                cut = slice(tile * LANES, (tile + 1) * LANES)
                inverse = cinv[tile:tile + 1, :]
                inner = isend[2, tile:tile + 1, :] * (inverse * inverse * inverse)
                value = inverse * total[:, t * LANES:(t + 1) * LANES] - sw[chip_rows, cut].astype(F32) * inner
                gwfull[k, 0, :, cut] = value[0:8]
                gwfull[k, 1, :, cut] = value[8:16]
        cols = pl.ds(j * 2 * CH, 2 * CH)
        send(gwfull.at[k, other, :, cols], gwfull.at[k, other, :, cols], gw_send.at[j], gw_recv.at[j], sibling)
        leaving.append((gwfull.at[k, other, :, cols], gw_send.at[j]))

    def inner_start(turn):
        for slot in (2, 1, 3):
            where = chip_at(0, slot) if turn == 0 else chip_at(slot, 0)
            send(isend.at[turn], irecv.at[turn, slot], inner_send.at[turn], inner_recv.at[turn], where)
        leaving.append((irecv.at[turn, pl.ds(1, 3)], inner_send.at[turn]))

    def inner_end(turn):
        await_bytes(irecv.at[turn, pl.ds(1, 3)], inner_recv.at[turn])
        isend[turn + 1] = isend[turn] + irecv[turn, 1] + irecv[turn, 2] + irecv[turn, 3]

    def feature_sibling():
        send(feat.at[half_rows(other)], fsib, feat_send.at[0], feat_recv.at[0], sibling)
        leaving.append((fsib, feat_send.at[0]))

    def share(where, half):
        return aligned(where * ZROWS + half * ZHALF, ZHALF)

    def feature_scatter():
        await_bytes(fsib, feat_recv.at[0])
        fsib[...] = feat[half_rows(k), :] + fsib[...]
        for half in range(2):
            for dz in Z_ORDER:
                to = lax.rem(z + dz, NZ)
                send(
                    fsib.at[pl.ds(share(to, half), ZHALF)], fz.at[half, dz],
                    feat_send.at[1 + half], feat_recv.at[1 + half], row_at(dz, 0),
                )
            leaving.append((fz.at[half, pl.ds(1, NZ - 1)], feat_send.at[1 + half]))

    def feature_gather(half):
        await_bytes(fz.at[half, pl.ds(1, NZ - 1)], feat_recv.at[1 + half])
        rows = pl.ds(share(z, half), ZHALF)
        feature = fsib[rows, :]
        for dz in range(1, NZ):
            feature = feature + fz[half, dz]
        rows_wide = srow[rows, :]
        inverse = rinv[rows, 0:1]
        rg[rows, :] = inverse * feature - rows_wide * (inverse * inverse * inverse) * jnp.sum(
            rows_wide * feature, axis=1, keepdims=True
        )
        for dz in Z_ORDER:
            send(rg.at[rows], rg.at[rows], feat_send.at[3 + half], feat_recv.at[3 + half], row_at(dz, 0))
        leaving.append((fz.at[half, pl.ds(1, NZ - 1)], feat_send.at[3 + half]))

    def feature_end(half):
        await_bytes(fz.at[half, pl.ds(1, NZ - 1)], feat_recv.at[3 + half])

    make_grad(0, 0)
    products(0, 0)
    first_opposite(0)
    first_direct(0)
    make_grad(1, 1)

    def gradient(j, carry):
        slot = lax.rem(j, 2)
        products(j, slot)
        make_grad(j + 1, 1 - slot)
        first_opposite(j)

        @pl.when(j < EARLY)
        def direct():
            first_direct(j)

        @pl.when(j >= LAG)
        def forward():
            first_forward(j - LAG, False)

        return carry

    lax.fori_loop(1, PAIRS - 1, gradient, 0)
    products(PAIRS - 1, (PAIRS - 1) % 2)
    feature_sibling()
    inner_start(0)
    first_opposite(PAIRS - 1)
    for j in range(PAIRS - 1 - LAG, PAIRS):
        first_forward(j, j >= EARLY)
        if j == PAIRS - 1 - LAG:
            feature_scatter()
    inner_end(0)
    inner_start(1)
    second_start(0)
    second_start(1)
    second_start(2)
    feature_gather(0)
    second_start(3)
    finish(0)
    finish(1)
    feature_gather(1)
    finish(2)
    finish(3)
    target_sum = row_sum * (row_scale * TOTAL_ROWS)
    target_logits = rows_end(4) * (row_scale * (TOTAL_ROWS / LOG2E))
    lossrow[...] = log_total * target_sum - target_logits
    loss_ref[...] = jnp.where(k == 0, lossrow[0:3, :], lossrow[3:6, :])
    feature_end(0)
    feature_end(1)
    rg_ref[...] = rg[...]
    for j in range(PAIRS):
        await_bytes(gwfull.at[other, k, :, pl.ds(j * 2 * CH, 2 * CH)], gw_recv.at[j])
    for core in range(NK):
        gw_ref[core] = gwfull[core, k]

    for ref, sem in leaving:
        await_bytes(ref, sem)

    def sent(q, carry):
        await_bytes(pg.at[q, pl.ds(0, 192)], rs_send.at[q, 0])
        await_bytes(second.at[q, pl.ds(0, 48)], rs_send.at[q, 1])
        return carry

    lax.fori_loop(0, PARTS, sent, 0)


def finish_kernel(midx, loss_part, gw_part, rg, loss_ref, gw_ref, gp_ref):
    for row in range(OWN // LANES):
        loss_ref[row * LANES:(row + 1) * LANES] = loss_part[row, :]
    for core in range(NK):
        gw_ref[:, core * COLS:(core + 1) * COLS] = gw_part[core]
    index = midx[...].reshape(1, OWN)
    patch_id = lax.broadcasted_iota(jnp.int32, (PATCH, OWN), 0)
    scatter = jnp.where(patch_id == index, 1.0, 0.0).astype(BF16)
    value = rg[...]
    high = value.astype(BF16)
    value = value - high.astype(F32)
    middle = value.astype(BF16)
    low = (value - middle.astype(F32)).astype(BF16)
    gp_ref[...] = (
        jnp.dot(scatter, low, preferred_element_type=F32)
        + jnp.dot(scatter, middle, preferred_element_type=F32)
        + jnp.dot(scatter, high, preferred_element_type=F32)
    )


def shards(teacher_patches, student_patches, mask_index, teacher_weight, student_weight):
    vmem = pl.BlockSpec(memory_space=pltpu.VMEM)
    hbm = pl.BlockSpec(memory_space=pl.ANY)
    dma = pltpu.SemaphoreType.DMA
    scratch = [
        pltpu.VMEM((PATCH, WIDTH), BF16),
        pltpu.VMEM((PATCH, WIDTH), BF16),
        pltpu.VMEM((WIDTH, COLS), BF16),
        pltpu.VMEM((WIDTH, COLS), BF16),
        pltpu.VMEM((WIDTH, COLS), BF16),
        pltpu.VMEM((WIDTH, COLS), BF16),
        pltpu.VMEM((TILES, LANES), F32),
        pltpu.VMEM((2, NK, OWN, WIDTH), F32),
        pltpu.VMEM((ROWS, WIDTH), BF16),
        pltpu.VMEM((ROWS, WIDTH), BF16),
        pltpu.VMEM((2, WIDTH, ROWS), BF16),
        pltpu.VMEM((OWN, WIDTH), F32),
        pltpu.VMEM((OWN, LANES), F32),
        pltpu.VMEM((ROWS, COLS), F32),
        pltpu.VMEM((ROWS, COLS), F32),
        pltpu.VMEM((ROWS, LANES), F32),
        pltpu.VMEM((ROWS, LANES), F32),
        pltpu.VMEM((3, TILES, LANES), F32),
        pltpu.VMEM((3, CHIPS, TILES, LANES), F32),
        pltpu.VMEM((TILES, LANES), F32),
        pltpu.VMEM((5, 8, LANES), F32),
        pltpu.VMEM((5, NZ * NK, 8, LANES), F32),
        pltpu.VMEM((ROWS, LANES), F32),
        pltpu.VMEM((ROWS, LANES), F32),
        pltpu.VMEM((2, ROWS, 2 * CH), BF16),
        pltpu.VMEM((PARTS, WIDTH, CH), F32),
        pltpu.VMEM((PARTS, 2, 32, CH), F32),
        pltpu.VMEM((PARTS, 2, 64, CH), F32),
        pltpu.VMEM((PARTS, 3, 16, CH), F32),
        pltpu.VMEM((PARTS, 64, CH), F32),
        pltpu.VMEM((ROWS, WIDTH), F32),
        pltpu.VMEM((OWN, WIDTH), F32),
        pltpu.VMEM((2, NZ, ZHALF, WIDTH), F32),
        pltpu.VMEM((OWN, WIDTH), F32),
        pltpu.VMEM((NK, NK, 8, COLS), F32),
        pltpu.VMEM((8, LANES), F32),
        pltpu.VMEM((3, TILES, LANES), F32),
        pltpu.VMEM((2, 4, TILES, LANES), F32),
        dma((4,)),
        dma((2,)),
        dma((2,)),
        dma((3, SPLIT)),
        dma((3, SPLIT)),
        dma((5,)),
        dma((5,)),
        dma((PARTS, 2)),
        dma((PARTS, 4)),
        dma((5,)),
        dma((5,)),
        dma((PAIRS,)),
        dma((PAIRS,)),
        dma((2,)),
        dma((2,)),
    ]
    loss_part, gw_part, row_grad = pl.pallas_call(
        kernel,
        out_shape=(
            jax.ShapeDtypeStruct((OWN // LANES, LANES), F32),
            jax.ShapeDtypeStruct((NK, WIDTH // DP, COLS), F32),
            jax.ShapeDtypeStruct((OWN, WIDTH), F32),
        ),
        in_specs=[hbm, hbm, vmem, hbm, hbm],
        out_specs=(vmem, vmem, vmem),
        scratch_shapes=scratch,
        compiler_params=pltpu.CompilerParams(
            collective_id=0, has_side_effects=True, vmem_limit_bytes=60 * 1024 * 1024
        ),
    )(teacher_patches, student_patches, mask_index, teacher_weight, student_weight)
    return pl.pallas_call(
        finish_kernel,
        out_shape=(
            jax.ShapeDtypeStruct((OWN,), F32),
            jax.ShapeDtypeStruct((WIDTH // DP, NK * COLS), F32),
            jax.ShapeDtypeStruct((PATCH, WIDTH), F32),
        ),
        in_specs=[vmem] * 4,
        out_specs=(vmem, vmem, vmem),
    )(mask_index, loss_part, gw_part, row_grad)


def solution(mesh):
    placed = (P("dp", None), P("dp", None), P("dp"), P(None, "proto"), P(None, "proto"))
    return jax.shard_map(
        shards,
        mesh=mesh,
        in_specs=placed,
        out_specs=(P("dp"), P("dp", "proto"), P("dp", None)),
        check_vma=False,
    )
```

```python
import math

import jax
import jax.numpy as jnp
from jax import lax
from jax.experimental import pallas as pl
from jax.experimental.pallas import tpu as pltpu
from jax.sharding import PartitionSpec as P

MESH = pl.DeviceIdType.MESH
F32 = jnp.float32
BF16 = jnp.bfloat16

EPS = 1e-06
TEACHER_TEMP = 0.07
STUDENT_TEMP = 0.1
LOG2E = 1.0 / math.log(2.0)

NY, NX, NK, NZ = 4, 4, 2, 8
DP = NY * NX * NK
CHIPS = NY * NX
OWN = 384
ROWS = NK * OWN
WIDTH = 256
PATCH = 768
COLS = 4096
LANES = 128
CH = 512
PARTS = COLS // CH
TOTAL_ROWS = OWN * DP
TOTAL_PROTOS = COLS * NK * NZ
ZROWS = OWN // NZ
GRAD_SCALE = 1.0 / (TOTAL_ROWS * STUDENT_TEMP)
COL_PEERS = [(dy, dx) for dy in range(NY) for dx in range(NX)]
ROW_PEERS = [(dz, dk) for dz in range(NZ) for dk in range(NK)]
PAIRS = PARTS // 2
TILES = COLS // LANES
SPLIT = 2
PIECE = TILES // SPLIT
RB = 128
STEP = 64
ZHALF = ZROWS // 2
LAG = 2
EARLY = PAIRS // 2


def farthest_first(peers, sizes):
    return sorted(enumerate(peers), key=lambda at: -sum(min(d, n - d) for d, n in zip(at[1], sizes)))[:-1]


COL_ORDER = farthest_first(COL_PEERS, (NY, NX))
ROW_ORDER = farthest_first(ROW_PEERS, (NZ, NK))
Z_ORDER = [4, 3, 5, 2, 6, 1, 7]


def aligned(value, unit):
    return pl.multiple_of(value, unit)


def kernel(
    tpat_hbm, spat_hbm, midx, tw_hbm, sw_hbm,
    loss_ref, gw_ref, rg_ref,
    tpat, spat, tw, sw, tp, sp, cinv, units, tu, su, sut, srow, rinv,
    e_ref, l_ref, part, part2, csend, crecv, cscale, rsend, rrecv, rcol, ltot,
    grad, pg, r1, r2, r4, second, feat, fsib, fz, rg, gwfull, lossrow,
    isend, irecv,
    load_sem, unit_send, unit_recv, col_send, col_recv, row_send, row_recv,
    rs_send, rs_recv, feat_send, feat_recv, gw_send, gw_recv, inner_send, inner_recv,
):
    dp = lax.axis_index("dp")
    z = lax.axis_index("proto")
    k = lax.rem(dp, NK)
    chip = lax.div(dp, NK)
    x = lax.rem(chip, NX)
    y = lax.div(chip, NX)
    other = lax.rem(k + 1, NK)

    def device(yy, xx, kk, zz):
        return ((yy * NX + xx) * NK + kk, zz)

    def chip_at(dy, dx):
        return device(lax.rem(y + dy, NY), lax.rem(x + dx, NX), k, z)

    def row_at(dz, dk):
        return device(y, x, lax.rem(k + dk, NK), lax.rem(z + dz, NZ))

    sibling = row_at(0, 1)

    def send(src, dst, send_sem, recv_sem, where):
        copy = pltpu.make_async_remote_copy(
            src_ref=src, dst_ref=dst, send_sem=send_sem, recv_sem=recv_sem,
            device_id=where, device_id_type=MESH,
        )
        copy.start()

    def await_bytes(ref, sem):
        pltpu.make_async_copy(ref, ref, sem).wait()

    leaving = []

    loads = []
    mine = pl.ds(aligned(k * COLS, COLS), COLS)
    for turn, (src, dst) in enumerate(
        ((tpat_hbm, tpat), (tw_hbm.at[:, mine], tw), (spat_hbm, spat), (sw_hbm.at[:, mine], sw))
    ):
        loads.append(pltpu.make_async_copy(src, dst, load_sem.at[turn]))
        loads[-1].start()

    barrier = pltpu.get_barrier_semaphore()
    for _, (dz, dk) in ROW_ORDER:
        pl.semaphore_signal(barrier, inc=1, device_id=row_at(dz, dk), device_id_type=MESH)
    for _, (dy, dx) in COL_ORDER:
        pl.semaphore_signal(barrier, inc=1, device_id=chip_at(dy, dx), device_id_type=MESH)

    def half_rows(core):
        return pl.ds(aligned(core * OWN, LANES), OWN)

    index = midx[...].reshape(1, OWN)
    index_col = jnp.transpose(jnp.broadcast_to(index.astype(F32), (LANES, OWN)))
    lane = lax.broadcasted_iota(jnp.int32, (OWN, LANES), 1).astype(F32)
    onehot = jnp.concatenate(
        [jnp.where(index_col == lane + float(t * LANES), 1.0, 0.0) for t in range(PATCH // LANES)], axis=1
    ).astype(BF16)

    def unit_rows(side, patches, ref):
        rows = jnp.dot(onehot, patches[...], preferred_element_type=F32)
        inverse = lax.rsqrt(jnp.sum(rows * rows, axis=1, keepdims=True) + EPS)
        unit = (rows * inverse).astype(BF16)
        ref[half_rows(k), :] = unit
        units[side, k] = unit.astype(F32)
        return rows, inverse

    loads[0].wait()
    unit_rows(0, tpat, tu)
    loads[2].wait()
    srow_value, sinv = unit_rows(1, spat, su)
    srow[...] = srow_value
    rinv[...] = jnp.broadcast_to(sinv, (OWN, LANES))

    def teacher_columns(j, carry):
        cols = pl.ds(aligned(j * CH, CH), CH)
        wide = tw[:, cols].astype(F32)
        inverse = lax.rsqrt(jnp.sum(wide * wide, axis=0, keepdims=True) + EPS)
        tp[:, cols] = (wide * inverse).astype(BF16)
        return carry

    def student_columns(j, carry):
        cols = pl.ds(aligned(j * CH, CH), CH)
        wide = sw[:, cols].astype(F32)
        inverse = lax.rsqrt(jnp.sum(wide * wide, axis=0, keepdims=True) + EPS)
        for t in range(CH // LANES):
            cinv[pl.ds(j * (CH // LANES) + t, 1), :] = inverse[:, t * LANES:(t + 1) * LANES]
        sp[:, cols] = (wide * inverse).astype(BF16)
        return carry

    def teacher_exp(core, first, last, add, blocks=range(OWN // RB)):
        def body(j, carry):
            cols = pl.ds(aligned(j * CH, CH), CH)
            total = jnp.zeros((1, CH), F32)
            for rb in blocks:
                at = pl.ds(aligned(core * OWN + rb * RB, RB), RB)
                value = jnp.exp2(
                    jnp.dot(tu[at, :], tp[:, cols], preferred_element_type=F32) * (LOG2E / TEACHER_TEMP)
                )
                e_ref[at, cols] = value
                total = total + jnp.sum(value, axis=0, keepdims=True)
            for t in range(CH // LANES):
                row = pl.ds(j * (CH // LANES) + t, 1)
                piece = total[:, t * LANES:(t + 1) * LANES]
                csend[0, row, :] = csend[0, row, :] + piece if add else piece
            return carry

        lax.fori_loop(first, last, body, 0)

    def student_logits(core):
        def body(j, carry):
            cols = pl.ds(aligned(j * CH, CH), CH)
            for rb in range(OWN // RB):
                at = pl.ds(aligned(core * OWN + rb * RB, RB), RB)
                value = jnp.dot(su[at, :], sp[:, cols], preferred_element_type=F32) * (LOG2E / STUDENT_TEMP)
                l_ref[at, cols] = value
                power = jnp.exp2(value)
                total = part2[at, :]
                for t in range(CH // LANES):
                    total = total + power[:, t * LANES:(t + 1) * LANES]
                part2[at, :] = total
            return carry

        lax.fori_loop(0, PARTS, body, 0)

    def columns_start(turn, piece):
        cut = pl.ds(piece * PIECE, PIECE)
        for slot, (dy, dx) in COL_ORDER:
            send(
                csend.at[turn, cut], crecv.at[turn, slot, cut],
                col_send.at[turn, piece], col_recv.at[turn, piece], chip_at(dy, dx),
            )
        leaving.append((crecv.at[turn, pl.ds(1, CHIPS - 1), cut], col_send.at[turn, piece]))

    def columns_end(turn, piece):
        cut = pl.ds(piece * PIECE, PIECE)
        await_bytes(crecv.at[turn, pl.ds(1, CHIPS - 1), cut], col_recv.at[turn, piece])
        total = csend[turn, cut, :]
        for slot in range(1, CHIPS):
            total = total + crecv[turn, slot, cut, :]
        cscale[cut, :] = 1.0 / (total * TOTAL_PROTOS)

    def rows_start(turn):
        for slot, (dz, dk) in ROW_ORDER:
            send(rsend.at[turn], rrecv.at[turn, slot], row_send.at[turn], row_recv.at[turn], row_at(dz, dk))
        leaving.append((rrecv.at[turn, pl.ds(1, NZ * NK - 1)], row_send.at[turn]))

    def rows_end(turn):
        await_bytes(rrecv.at[turn, pl.ds(1, NZ * NK - 1)], row_recv.at[turn])
        total = rsend[turn]
        for slot in range(1, NZ * NK):
            total = total + rrecv[turn, slot]
        return total

    def to_column(ref, rows):
        for b in range(ROWS // LANES):
            ref[b * LANES:(b + 1) * LANES, :] = jnp.transpose(jnp.broadcast_to(rows[b:b + 1, :], (LANES, LANES)))

    def lane_sums(turn, ref):
        for b in range(ROWS // LANES):
            rsend[turn, b:b + 1, :] = jnp.sum(
                jnp.transpose(ref[b * LANES:(b + 1) * LANES, :]), axis=0, keepdims=True
            )

    def row_pass(piece):
        def body(rb, carry):
            at = pl.ds(aligned(rb * STEP, STEP), STEP)
            total = part[at, :] if piece else jnp.zeros((STEP, LANES), F32)
            for t in range(piece * PIECE, (piece + 1) * PIECE):
                cut = slice(t * LANES, (t + 1) * LANES)
                total = total + e_ref[at, cut] * cscale[t:t + 1, :]
            part[at, :] = total
            return carry

        lax.fori_loop(0, ROWS // STEP, body, 0)

    def cross_pass():
        def body(rb, carry):
            at = pl.ds(aligned(rb * STEP, STEP), STEP)
            total = jnp.zeros((STEP, LANES), F32)
            for t in range(TILES):
                cut = slice(t * LANES, (t + 1) * LANES)
                total = total + e_ref[at, cut] * cscale[t:t + 1, :] * l_ref[at, cut]
            part2[at, :] = total
            return carry

        lax.fori_loop(0, ROWS // STEP, body, 0)

    def col_pass(turn, piece):
        def body(rb, totals):
            at = pl.ds(aligned(rb * STEP, STEP), STEP)
            scale = rcol[at, :]
            out = []
            for t in range(PIECE):
                cut = slice((piece * PIECE + t) * LANES, (piece * PIECE + t + 1) * LANES)
                value = e_ref[at, cut] * scale
                out.append(totals[t] + jnp.sum(value.reshape(STEP // 8, 8, LANES), axis=0))
            return tuple(out)

        totals = lax.fori_loop(0, ROWS // STEP, body, tuple(jnp.zeros((8, LANES), F32) for _ in range(PIECE)))
        for t in range(PIECE):
            row = piece * PIECE + t
            csend[turn, row:row + 1, :] = jnp.sum(totals[t], axis=0, keepdims=True)

    loads[1].wait()
    lax.fori_loop(0, PARTS, teacher_columns, 0)
    teacher_exp(k, 0, PARTS, False)
    part2[...] = jnp.zeros_like(part2)
    rsend[...] = jnp.zeros_like(rsend)

    pl.semaphore_wait(barrier, CHIPS - 1 + NZ * NK - 1)
    blocks = [(0, rb * RB, RB) for rb in range(OWN // RB)] + [(1, 0, OWN)]
    for turn, (side, at, depth) in enumerate(blocks):
        piece = units.at[side, k, pl.ds(at, depth)]
        send(piece, piece, unit_send.at[turn], unit_recv.at[turn], sibling)
        leaving.append((piece, unit_send.at[turn]))
    loads[3].wait()
    lax.fori_loop(0, PARTS, student_columns, 0)
    for piece in range(SPLIT):
        for rb in range(OWN // RB):
            if piece == 0:
                rows = pl.ds(rb * RB, RB)
                await_bytes(units.at[0, other, rows], unit_recv.at[rb])
                tu[pl.ds(aligned(other * OWN + rb * RB, RB), RB), :] = units[0, other, rows, :].astype(BF16)
            teacher_exp(other, piece * PARTS // SPLIT, (piece + 1) * PARTS // SPLIT, True, (rb,))
        columns_start(0, piece)
    await_bytes(units.at[1, other], unit_recv.at[OWN // RB])
    su[half_rows(other), :] = units[1, other].astype(BF16)
    student_logits(k)
    student_logits(other)
    for piece in range(SPLIT):
        columns_end(0, piece)
        row_pass(piece)
    lane_sums(0, part)
    rows_start(0)
    lane_sums(3, part2)
    rows_start(3)
    for core in range(NK):
        sut[1, :, core * OWN:(core + 1) * OWN] = jnp.transpose(units[1, core]).astype(BF16)
    for xx in range(NX):
        for yy in range(NY):
            to, at = (xx * NY + yy) * 16, (yy * NX + xx) * 16
            sut[0, to:to + 16, :] = sut[1, at:at + 16, :]
    to_column(rcol, 1.0 / (rows_end(0) * TOTAL_ROWS))
    for piece in range(SPLIT):
        col_pass(1, piece)
        columns_start(1, piece)
    log_total = jnp.log(rows_end(3))
    to_column(ltot, (log_total - math.log(GRAD_SCALE)) * LOG2E)
    for piece in range(SPLIT):
        columns_end(1, piece)
        row_pass(piece)
    lane_sums(1, part)
    rows_start(1)
    to_column(rcol, 1.0 / (rows_end(1) * TOTAL_ROWS))
    for piece in range(SPLIT):
        col_pass(2, piece)
        columns_start(2, piece)
    for piece in range(SPLIT):
        columns_end(2, piece)
        row_pass(piece)
    lane_sums(2, part)
    rows_start(2)
    cross_pass()
    lane_sums(4, part2)
    rows_start(4)
    row_sum = rows_end(2)
    row_scale = 1.0 / (row_sum * TOTAL_ROWS)
    to_column(rcol, row_scale * (TOTAL_ROWS * GRAD_SCALE))

    ahead = {0: (chip_at(0, 1), chip_at(0, 3), x), 1: (chip_at(1, 0), chip_at(3, 0), y)}
    across = {0: chip_at(0, 2), 1: chip_at(2, 0)}
    feat[...] = jnp.zeros_like(feat)

    def make_grad(j, slot):
        for rb in range(ROWS // STEP):
            at = slice(rb * STEP, (rb + 1) * STEP)
            scale = rcol[at, :]
            shift = ltot[at, :]
            for t in range(2 * CH // LANES):
                tile = j * (2 * CH // LANES) + t
                cut = pl.ds(aligned(tile * LANES, LANES), LANES)
                probs = jnp.exp2(l_ref[at, cut] - shift)
                target = e_ref[at, cut] * cscale[pl.ds(tile, 1), :] * scale
                grad[slot, at, t * LANES:(t + 1) * LANES] = (probs - target).astype(BF16)

    def products(j, slot):
        for kind in range(2):
            q = 2 * j + kind
            value = jnp.dot(sut[kind], grad[slot, :, kind * CH:(kind + 1) * CH], preferred_element_type=F32)
            pg[q] = value
            for t in range(CH // LANES):
                cut = pl.ds(aligned(q * CH + t * LANES, LANES), LANES)
                inner = jnp.zeros((16, LANES), F32)
                for yy in range(NY):
                    for xx in range(NX):
                        at = (yy * NX + xx) * 16
                        to = (xx * NY + yy) * 16 if kind == 0 else at
                        inner = inner + (
                            sw[at:at + 16, cut].astype(F32) * value[to:to + 16, t * LANES:(t + 1) * LANES]
                        )
                isend[0, pl.ds(q * (CH // LANES) + t, 1), :] = jnp.sum(inner, axis=0, keepdims=True)
        cols = pl.ds(aligned(j * 2 * CH, 2 * CH), 2 * CH)
        feat[...] += lax.dot_general(
            grad[slot], sp[:, cols], (((1,), (1,)), ((), ())), preferred_element_type=F32
        )

    def first_opposite(j):
        for kind in range(2):
            q = 2 * j + kind
            plus, minus, a = ahead[kind]
            opposite = lax.rem(a + 2, 4) * 64
            send(pg.at[q, pl.ds(aligned(opposite, 32), 32)], r1.at[q, 0], rs_send.at[q, 0], rs_recv.at[q, 0], plus)
            send(pg.at[q, pl.ds(aligned(opposite + 32, 32), 32)], r1.at[q, 1], rs_send.at[q, 0], rs_recv.at[q, 1], minus)

    def first_direct(j):
        for kind in range(2):
            q = 2 * j + kind
            plus, minus, a = ahead[kind]
            ap, am = lax.rem(a + 1, 4) * 64, lax.rem(a + 3, 4) * 64
            send(pg.at[q, pl.ds(aligned(ap + 32, 32), 32)], r2.at[q, 0, pl.ds(32, 32)], rs_send.at[q, 0], rs_recv.at[q, 2], plus)
            send(pg.at[q, pl.ds(aligned(am, 32), 32)], r2.at[q, 1, pl.ds(0, 32)], rs_send.at[q, 0], rs_recv.at[q, 2], minus)

    def first_forward(j, whole):
        for kind in range(2):
            q = 2 * j + kind
            plus, minus, a = ahead[kind]
            ap = aligned(lax.rem(a + 1, 4) * 64, 64)
            am = aligned(lax.rem(a + 3, 4) * 64, 64)
            low, high = pl.ds(ap, 32), pl.ds(aligned(am + 32, 32), 32)
            await_bytes(r1.at[q, 0], rs_recv.at[q, 0])
            pg[q, low, :] = pg[q, low, :] + r1[q, 0]
            if whole:
                send(pg.at[q, pl.ds(ap, 64)], r2.at[q, 0], rs_send.at[q, 0], rs_recv.at[q, 2], plus)
            else:
                send(pg.at[q, low], r2.at[q, 0, pl.ds(0, 32)], rs_send.at[q, 0], rs_recv.at[q, 2], plus)
            await_bytes(r1.at[q, 1], rs_recv.at[q, 1])
            pg[q, high, :] = pg[q, high, :] + r1[q, 1]
            if whole:
                send(pg.at[q, pl.ds(am, 64)], r2.at[q, 1], rs_send.at[q, 0], rs_recv.at[q, 2], minus)
            else:
                send(pg.at[q, high], r2.at[q, 1, pl.ds(32, 32)], rs_send.at[q, 0], rs_recv.at[q, 2], minus)

    def second_start(j):
        for kind in range(2):
            q = 2 * j + kind
            a = ahead[kind][2]
            plus, minus, b = ahead[1 - kind]
            await_bytes(r2.at[q], rs_recv.at[q, 2])
            second[q] = pg[q, pl.ds(aligned(a * 64, 64), 64), :] + r2[q, 0] + r2[q, 1]
            for slot, where in ((2, across[1 - kind]), (0, plus), (1, minus)):
                block = pl.ds(aligned(lax.rem(b + (1, 3, 2)[slot], 4) * 16, 16), 16)
                send(second.at[q, block], r4.at[q, slot], rs_send.at[q, 1], rs_recv.at[q, 3], where)

    chip_rows = pl.ds(aligned(chip * 16, 16), 16)

    def finish(j):
        if j == 0:
            inner_end(1)
        for kind in range(2):
            q = 2 * j + kind
            b = ahead[1 - kind][2]
            await_bytes(r4.at[q], rs_recv.at[q, 3])
            total = second[q, pl.ds(aligned(b * 16, 16), 16), :] + r4[q, 0] + r4[q, 1] + r4[q, 2]
            for t in range(CH // LANES):
                tile = q * (CH // LANES) + t
                cut = slice(tile * LANES, (tile + 1) * LANES)
                inverse = cinv[tile:tile + 1, :]
                inner = isend[2, tile:tile + 1, :] * (inverse * inverse * inverse)
                value = inverse * total[:, t * LANES:(t + 1) * LANES] - sw[chip_rows, cut].astype(F32) * inner
                gwfull[k, 0, :, cut] = value[0:8]
                gwfull[k, 1, :, cut] = value[8:16]
        cols = pl.ds(j * 2 * CH, 2 * CH)
        send(gwfull.at[k, other, :, cols], gwfull.at[k, other, :, cols], gw_send.at[j], gw_recv.at[j], sibling)
        leaving.append((gwfull.at[k, other, :, cols], gw_send.at[j]))

    def inner_start(turn):
        for slot in (2, 1, 3):
            where = chip_at(0, slot) if turn == 0 else chip_at(slot, 0)
            send(isend.at[turn], irecv.at[turn, slot], inner_send.at[turn], inner_recv.at[turn], where)
        leaving.append((irecv.at[turn, pl.ds(1, 3)], inner_send.at[turn]))

    def inner_end(turn):
        await_bytes(irecv.at[turn, pl.ds(1, 3)], inner_recv.at[turn])
        isend[turn + 1] = isend[turn] + irecv[turn, 1] + irecv[turn, 2] + irecv[turn, 3]

    def feature_sibling():
        send(feat.at[half_rows(other)], fsib, feat_send.at[0], feat_recv.at[0], sibling)
        leaving.append((fsib, feat_send.at[0]))

    def share(where, half):
        return aligned(where * ZROWS + half * ZHALF, ZHALF)

    def feature_scatter():
        await_bytes(fsib, feat_recv.at[0])
        fsib[...] = feat[half_rows(k), :] + fsib[...]
        for half in range(2):
            for dz in Z_ORDER:
                to = lax.rem(z + dz, NZ)
                send(
                    fsib.at[pl.ds(share(to, half), ZHALF)], fz.at[half, dz],
                    feat_send.at[1 + half], feat_recv.at[1 + half], row_at(dz, 0),
                )
            leaving.append((fz.at[half, pl.ds(1, NZ - 1)], feat_send.at[1 + half]))

    def feature_gather(half):
        await_bytes(fz.at[half, pl.ds(1, NZ - 1)], feat_recv.at[1 + half])
        rows = pl.ds(share(z, half), ZHALF)
        feature = fsib[rows, :]
        for dz in range(1, NZ):
            feature = feature + fz[half, dz]
        rows_wide = srow[rows, :]
        inverse = rinv[rows, 0:1]
        rg[rows, :] = inverse * feature - rows_wide * (inverse * inverse * inverse) * jnp.sum(
            rows_wide * feature, axis=1, keepdims=True
        )
        for dz in Z_ORDER:
            send(rg.at[rows], rg.at[rows], feat_send.at[3 + half], feat_recv.at[3 + half], row_at(dz, 0))
        leaving.append((fz.at[half, pl.ds(1, NZ - 1)], feat_send.at[3 + half]))

    def feature_end(half):
        await_bytes(fz.at[half, pl.ds(1, NZ - 1)], feat_recv.at[3 + half])

    make_grad(0, 0)
    products(0, 0)
    first_opposite(0)
    first_direct(0)
    make_grad(1, 1)

    def gradient(j, carry):
        slot = lax.rem(j, 2)
        products(j, slot)
        make_grad(j + 1, 1 - slot)
        first_opposite(j)

        @pl.when(j < EARLY)
        def direct():
            first_direct(j)

        @pl.when(j >= LAG)
        def forward():
            first_forward(j - LAG, False)

        return carry

    lax.fori_loop(1, PAIRS - 1, gradient, 0)
    products(PAIRS - 1, (PAIRS - 1) % 2)
    feature_sibling()
    inner_start(0)
    first_opposite(PAIRS - 1)
    for j in range(PAIRS - 1 - LAG, PAIRS):
        first_forward(j, j >= EARLY)
        if j == PAIRS - 1 - LAG:
            feature_scatter()
    inner_end(0)
    inner_start(1)
    second_start(0)
    second_start(1)
    second_start(2)
    feature_gather(0)
    second_start(3)
    finish(0)
    finish(1)
    feature_gather(1)
    finish(2)
    finish(3)
    target_sum = row_sum * (row_scale * TOTAL_ROWS)
    target_logits = rows_end(4) * (row_scale * (TOTAL_ROWS / LOG2E))
    lossrow[...] = log_total * target_sum - target_logits
    loss_ref[...] = jnp.where(k == 0, lossrow[0:3, :], lossrow[3:6, :])
    feature_end(0)
    feature_end(1)
    rg_ref[...] = rg[...]
    for j in range(PAIRS):
        await_bytes(gwfull.at[other, k, :, pl.ds(j * 2 * CH, 2 * CH)], gw_recv.at[j])
    for core in range(NK):
        gw_ref[core] = gwfull[core, k]

    for ref, sem in leaving:
        await_bytes(ref, sem)

    def sent(q, carry):
        await_bytes(pg.at[q, pl.ds(0, 192)], rs_send.at[q, 0])
        await_bytes(second.at[q, pl.ds(0, 48)], rs_send.at[q, 1])
        return carry

    lax.fori_loop(0, PARTS, sent, 0)


def finish_kernel(midx, loss_part, gw_part, rg, loss_ref, gw_ref, gp_ref):
    for row in range(OWN // LANES):
        loss_ref[row * LANES:(row + 1) * LANES] = loss_part[row, :]
    for core in range(NK):
        gw_ref[:, core * COLS:(core + 1) * COLS] = gw_part[core]
    index = midx[...].reshape(1, OWN)
    patch_id = lax.broadcasted_iota(jnp.int32, (PATCH, OWN), 0)
    scatter = jnp.where(patch_id == index, 1.0, 0.0).astype(BF16)
    value = rg[...]
    high = value.astype(BF16)
    value = value - high.astype(F32)
    middle = value.astype(BF16)
    low = (value - middle.astype(F32)).astype(BF16)
    gp_ref[...] = (
        jnp.dot(scatter, low, preferred_element_type=F32)
        + jnp.dot(scatter, middle, preferred_element_type=F32)
        + jnp.dot(scatter, high, preferred_element_type=F32)
    )


def shards(teacher_patches, student_patches, mask_index, teacher_weight, student_weight):
    vmem = pl.BlockSpec(memory_space=pltpu.VMEM)
    hbm = pl.BlockSpec(memory_space=pl.ANY)
    dma = pltpu.SemaphoreType.DMA
    scratch = [
        pltpu.VMEM((PATCH, WIDTH), BF16),
        pltpu.VMEM((PATCH, WIDTH), BF16),
        pltpu.VMEM((WIDTH, COLS), BF16),
        pltpu.VMEM((WIDTH, COLS), BF16),
        pltpu.VMEM((WIDTH, COLS), BF16),
        pltpu.VMEM((WIDTH, COLS), BF16),
        pltpu.VMEM((TILES, LANES), F32),
        pltpu.VMEM((2, NK, OWN, WIDTH), F32),
        pltpu.VMEM((ROWS, WIDTH), BF16),
        pltpu.VMEM((ROWS, WIDTH), BF16),
        pltpu.VMEM((2, WIDTH, ROWS), BF16),
        pltpu.VMEM((OWN, WIDTH), F32),
        pltpu.VMEM((OWN, LANES), F32),
        pltpu.VMEM((ROWS, COLS), F32),
        pltpu.VMEM((ROWS, COLS), F32),
        pltpu.VMEM((ROWS, LANES), F32),
        pltpu.VMEM((ROWS, LANES), F32),
        pltpu.VMEM((3, TILES, LANES), F32),
        pltpu.VMEM((3, CHIPS, TILES, LANES), F32),
        pltpu.VMEM((TILES, LANES), F32),
        pltpu.VMEM((5, 8, LANES), F32),
        pltpu.VMEM((5, NZ * NK, 8, LANES), F32),
        pltpu.VMEM((ROWS, LANES), F32),
        pltpu.VMEM((ROWS, LANES), F32),
        pltpu.VMEM((2, ROWS, 2 * CH), BF16),
        pltpu.VMEM((PARTS, WIDTH, CH), F32),
        pltpu.VMEM((PARTS, 2, 32, CH), F32),
        pltpu.VMEM((PARTS, 2, 64, CH), F32),
        pltpu.VMEM((PARTS, 3, 16, CH), F32),
        pltpu.VMEM((PARTS, 64, CH), F32),
        pltpu.VMEM((ROWS, WIDTH), F32),
        pltpu.VMEM((OWN, WIDTH), F32),
        pltpu.VMEM((2, NZ, ZHALF, WIDTH), F32),
        pltpu.VMEM((OWN, WIDTH), F32),
        pltpu.VMEM((NK, NK, 8, COLS), F32),
        pltpu.VMEM((8, LANES), F32),
        pltpu.VMEM((3, TILES, LANES), F32),
        pltpu.VMEM((2, 4, TILES, LANES), F32),
        dma((4,)),
        dma((4,)),
        dma((4,)),
        dma((3, SPLIT)),
        dma((3, SPLIT)),
        dma((5,)),
        dma((5,)),
        dma((PARTS, 2)),
        dma((PARTS, 4)),
        dma((5,)),
        dma((5,)),
        dma((PAIRS,)),
        dma((PAIRS,)),
        dma((2,)),
        dma((2,)),
    ]
    loss_part, gw_part, row_grad = pl.pallas_call(
        kernel,
        out_shape=(
            jax.ShapeDtypeStruct((OWN // LANES, LANES), F32),
            jax.ShapeDtypeStruct((NK, WIDTH // DP, COLS), F32),
            jax.ShapeDtypeStruct((OWN, WIDTH), F32),
        ),
        in_specs=[hbm, hbm, vmem, hbm, hbm],
        out_specs=(vmem, vmem, vmem),
        scratch_shapes=scratch,
        compiler_params=pltpu.CompilerParams(
            collective_id=0, has_side_effects=True, vmem_limit_bytes=60 * 1024 * 1024
        ),
    )(teacher_patches, student_patches, mask_index, teacher_weight, student_weight)
    return pl.pallas_call(
        finish_kernel,
        out_shape=(
            jax.ShapeDtypeStruct((OWN,), F32),
            jax.ShapeDtypeStruct((WIDTH // DP, NK * COLS), F32),
            jax.ShapeDtypeStruct((PATCH, WIDTH), F32),
        ),
        in_specs=[vmem] * 4,
        out_specs=(vmem, vmem, vmem),
    )(mask_index, loss_part, gw_part, row_grad)


def solution(mesh):
    placed = (P("dp", None), P("dp", None), P("dp"), P(None, "proto"), P(None, "proto"))
    return jax.shard_map(
        shards,
        mesh=mesh,
        in_specs=placed,
        out_specs=(P("dp"), P("dp", "proto"), P("dp", None)),
        check_vma=False,
    )
```
